256 devices in a mesh: seq: 16 (over x, y), nbr: 16 (over z, core).
Axes of the slice: x: 4, y: 4, z: 8, core: 2. Of those that a mesh axis runs over, the one named last changes fastest.
Arguments:
- tokens: bfloat16 [8192, 4096], P(('seq', 'nbr')), may hold values from -7 to 7
- nbr_embed: bfloat16 [256, 128, 896], P('seq', 'nbr'), may hold values from -7 to 7
- neighbour_table: int32 [128, 2], P('seq'), may hold values from 0 to 255, as said below
- valid_counts: int32 [128], replicated, may hold values from 1 to 2
- dec_proj: bfloat16 [4096, 3, 4096], P(None, None, 'nbr'), may hold values from -1 to 1
- enc_query: bfloat16 [896, 4096], P(None, 'nbr'), may hold values from -2 to 2
- enc_out: bfloat16 [4096, 896], P('nbr'), may hold values from -0.09375 to 0.09375
- enc_gain: float32 [896], replicated, may hold values from 0.1 to 1.9
- nbr_proj: bfloat16 [896, 2, 4096], P(None, None, 'nbr'), may hold values from -2 to 2
- out_proj: bfloat16 [4096, 4096], P('nbr'), may hold values from -0.09375 to 0.09375
Outputs:
- cross_out: bfloat16 [8192, 4096], P(('seq', 'nbr'))
- encoded: bfloat16 [32768, 896], P(('seq', 'nbr'))
The draws below stay inside these ranges and needn't reach their ends.
Inputs may be any that keep to these rules, and one draw needn't show every extreme that they name: `neighbour_table`: for each block b of 8 groups in order, the entries of those groups are a permutation of the neighbour rows b * 16 to (b + 1) * 16 - 1.
All inputs are finite; a program needn't handle non-finite values.
Results may differ from the reference program's by a relative error of at most 0.025.
Values may be sent and summed in bfloat16 or wider, within the bound.
A program may use at most 128 MiB of HBM per device.

```python
import math
import jax
import jax.numpy as jnp
from jax import lax

D = 4096
HEADS = 32
HEAD_DIM = 128
DE = 896
GROUP = 64
NLEN = 128
KN = 2
SEQ_LEN = 2048
CH_GRP = 8
NB_GRP = 16
TOKENS = 8192
GROUPS = 128
NBRS = 256


def draw_neighbour_table(key, part):
    blocks = GROUPS // CH_GRP
    block_keys = jax.random.split(jax.random.fold_in(key, 17), blocks)
    orders = jax.vmap(lambda block_key: jax.random.permutation(block_key, NB_GRP))(block_keys)
    offsets = jnp.arange(blocks, dtype=jnp.int32)[:, None] * NB_GRP
    return (orders.astype(jnp.int32) + offsets).reshape(GROUPS, KN).astype(jnp.int32)


def draw_tokens(key, part):
    values = jnp.clip(jax.random.normal(jax.random.fold_in(key, 21), (TOKENS, D), jnp.float32), -6.0, 6.0)
    return values.astype(jnp.bfloat16)


def draw_nbr_embed(key, part):
    values = jnp.clip(jax.random.normal(jax.random.fold_in(key, 31), (NBRS, NLEN, DE), jnp.float32), -6.0, 6.0)
    return values.astype(jnp.bfloat16)


def draw_dec_proj(key, part):
    values = jnp.clip(jax.random.normal(jax.random.fold_in(key, 41), (D, 3, HEADS * HEAD_DIM), jnp.float32), -4.0, 4.0) / math.sqrt(D)
    return values.astype(jnp.bfloat16)


def draw_enc_query(key, part):
    values = jnp.clip(jax.random.normal(jax.random.fold_in(key, 51), (DE, HEADS * HEAD_DIM), jnp.float32), -4.0, 4.0) / math.sqrt(DE)
    return values.astype(jnp.bfloat16)


def draw_nbr_proj(key, part):
    values = jnp.clip(jax.random.normal(jax.random.fold_in(key, 61), (DE, 2, HEADS * HEAD_DIM), jnp.float32), -4.0, 4.0) / math.sqrt(DE)
    return values.astype(jnp.bfloat16)


def plant(drawn, rng, smallest, largest):
    spot = [jax.random.randint(jax.random.fold_in(rng, axis), (), 0, length) for axis, length in enumerate(drawn.shape)]
    longest = drawn.shape.index(max(drawn.shape))
    beside = spot[:longest] + [(spot[longest] + 1) % drawn.shape[longest]] + spot[longest + 1:]
    return drawn.at[tuple(spot)].set(smallest).at[tuple(beside)].set(largest)


def steps_of(stream_key, extent, pieces, smallest, largest):
    gain, own = 1.0, jax.random.fold_in(stream_key, 6)
    for position, blocks in pieces:
        steps = jnp.exp(jax.random.uniform(jax.random.fold_in(own, position), (blocks,), jnp.float32, smallest / len(pieces), largest / len(pieces)))
        gain = gain * jnp.repeat(steps, extent[position] // blocks).reshape([-1 if axis == position else 1 for axis in range(len(extent))])
    return gain


def normal_values(stream_key, dims, deviation, limit, cuts=(), kind=jnp.bfloat16):
    entries = jax.random.normal(stream_key, dims, jnp.float32) * deviation
    if len(cuts) > 0:
        entries = steps_of(stream_key, dims, cuts, -0.22, 0.18) * entries
    return jnp.clip(entries, min=-limit, max=limit).astype(kind)


def setup_inputs(seed: int = 0) -> dict:
    streams_of = jax.random.split(jax.random.key(seed), 11)
    return {
        "tokens": draw_tokens(jax.random.fold_in(streams_of[10], 71), 0),
        "nbr_embed": draw_nbr_embed(jax.random.fold_in(streams_of[10], 71), 0),
        "neighbour_table": draw_neighbour_table(jax.random.fold_in(streams_of[10], 71), 0),
        "valid_counts": plant(jax.random.randint(streams_of[3], (GROUPS,), 1, KN + 1), jax.random.fold_in(streams_of[3], 1), 1, KN).astype(jnp.int32),
        "dec_proj": draw_dec_proj(jax.random.fold_in(streams_of[10], 71), 0),
        "enc_query": draw_enc_query(jax.random.fold_in(streams_of[10], 71), 0),
        "enc_out": normal_values(streams_of[6], (HEADS * HEAD_DIM, DE), (HEADS * HEAD_DIM) ** -0.5, 0.09375, ((0, 16),)),
        "enc_gain": jnp.clip(1.0 + 0.18 * jax.random.normal(streams_of[7], (DE,), jnp.float32), 0.1, 1.9),
        "nbr_proj": draw_nbr_proj(jax.random.fold_in(streams_of[10], 71), 0),
        "out_proj": normal_values(streams_of[9], (HEADS * HEAD_DIM, D), (HEADS * HEAD_DIM) ** -0.5, 0.09375, ((0, 16),)),
    }


def plain_softmax(scores):
    peak = lax.optimization_barrier(jnp.max(scores, axis=-1, keepdims=True))
    raised = jnp.exp(scores - peak)
    return (raised / lax.optimization_barrier(jnp.sum(raised, axis=-1, keepdims=True))).astype(jnp.bfloat16)

def masked_softmax(scores, allowed):
    live = jnp.any(allowed, axis=-1, keepdims=True)
    peak = lax.optimization_barrier(jnp.max(jnp.where(allowed, scores, -1e+30), axis=-1, keepdims=True))
    peak = jnp.where(live, peak, 0.0)
    raised = jnp.where(allowed, jnp.exp(scores - peak), 0.0)
    denominator = jnp.where(live, lax.optimization_barrier(jnp.sum(raised, axis=-1, keepdims=True)), 1.0)
    return (raised / denominator).astype(jnp.bfloat16)

def reference(tokens, nbr_embed, neighbour_table, valid_counts, dec_proj, enc_query, enc_out, enc_gain, nbr_proj, out_proj):
    all_width = HEADS * HEAD_DIM
    scale = 1.0 / HEAD_DIM ** 0.5
    projected = jnp.dot(tokens, dec_proj.reshape(D, 3 * all_width), preferred_element_type=jnp.float32).astype(jnp.bfloat16)
    projected = projected.reshape(TOKENS, 3, HEADS, HEAD_DIM)
    queries = projected[:, 0]
    cond_key = projected[:, 1].reshape(GROUPS, GROUP, HEADS, HEAD_DIM)
    cond_value = projected[:, 2].reshape(GROUPS, GROUP, HEADS, HEAD_DIM)
    row_ids = neighbour_table.reshape(-1).astype(jnp.int32)
    ordered = jnp.take(nbr_embed, row_ids, axis=0).reshape(GROUPS * KN * NLEN, DE)
    enc_queries = jnp.dot(ordered, enc_query, preferred_element_type=jnp.float32).astype(jnp.bfloat16)
    enc_queries = enc_queries.reshape(GROUPS, KN * NLEN, HEADS, HEAD_DIM)

    def enc_block(operands):
        block_query, block_key, block_value = operands
        scores = jnp.einsum('qhd,khd->hqk', block_query.astype(jnp.float32), block_key.astype(jnp.float32)) * scale
        weights = plain_softmax(scores)
        return jnp.einsum('hqk,khd->qhd', weights.astype(jnp.float32), block_value.astype(jnp.float32)).astype(jnp.bfloat16)
    enc_att = lax.map(enc_block, (enc_queries, cond_key, cond_value)).reshape(GROUPS * KN * NLEN, all_width)
    enc_sum = jnp.dot(enc_att, enc_out, preferred_element_type=jnp.float32)
    combined = ordered.astype(jnp.float32) + enc_sum
    encoded = (combined * lax.rsqrt(lax.optimization_barrier(jnp.mean(combined * combined, axis=-1, keepdims=True)) + 1e-06) * enc_gain).astype(jnp.bfloat16)
    nbr_kv = jnp.dot(encoded, nbr_proj.reshape(DE, 2 * all_width), preferred_element_type=jnp.float32).astype(jnp.bfloat16)
    nbr_kv = nbr_kv.reshape(GROUPS, KN * NLEN, 2, HEADS, HEAD_DIM)
    kv_ext = jnp.concatenate([jnp.zeros((1, KN * NLEN, 2, HEADS, HEAD_DIM), jnp.bfloat16), nbr_kv], axis=0)
    counts_ext = jnp.concatenate([jnp.zeros((1,), jnp.int32), valid_counts.astype(jnp.int32)], axis=0)
    query_pad = jnp.concatenate([jnp.zeros((1, HEADS, HEAD_DIM), jnp.bfloat16), queries, jnp.zeros((GROUP - 1, HEADS, HEAD_DIM), jnp.bfloat16)], axis=0)
    query_pad = query_pad.reshape(GROUPS + 1, GROUP, HEADS, HEAD_DIM)
    token_ids = jnp.arange((GROUPS + 1) * GROUP, dtype=jnp.int32) - 1
    active = (token_ids >= 0) & (token_ids < TOKENS) & (token_ids % SEQ_LEN >= GROUP - 1)
    active = active.reshape(GROUPS + 1, GROUP)
    key_slot = jnp.arange(KN * NLEN, dtype=jnp.int32) // NLEN

    def cca_block(operands):
        block_query, block_kv, block_count, block_active = operands
        scores = jnp.einsum('qhd,khd->hqk', block_query.astype(jnp.float32), block_kv[:, 0].astype(jnp.float32)) * scale
        allowed = block_active[None, :, None] & (key_slot < block_count)[None, None, :]
        weights = masked_softmax(scores, allowed)
        return jnp.einsum('hqk,khd->qhd', weights.astype(jnp.float32), block_kv[:, 1].astype(jnp.float32)).astype(jnp.bfloat16)
    cca_att = lax.map(cca_block, (query_pad, kv_ext, counts_ext, active))
    cca_att = cca_att.reshape((GROUPS + 1) * GROUP, all_width)[1:TOKENS + 1]
    cross_out = jnp.dot(cca_att, out_proj, preferred_element_type=jnp.float32).astype(jnp.bfloat16)
    return (cross_out, encoded)
```

```python
import jax
import jax.numpy as jnp
from jax import lax
from jax.experimental import pallas as pl
from jax.experimental.pallas import tpu as pltpu
from jax.sharding import PartitionSpec as P

HEAD_DIM = 128
GROUP = 64
NLEN = 128
SEQ_LEN = 2048
CHIPS = 8
F32 = jnp.float32
BF16 = jnp.bfloat16
MESH = pl.DeviceIdType.MESH


def dot(a, b):
    return jnp.dot(a, b, preferred_element_type=F32)


def dot_t(a, b):
    return lax.dot_general(a, b, (((1,), (1,)), ((), ())), preferred_element_type=F32)


def softmax(scores):
    peak = jnp.max(scores, axis=-1, keepdims=True)
    raised = jnp.exp(scores - peak)
    return (raised * (1.0 / jnp.sum(raised, axis=-1, keepdims=True))).astype(BF16)


def wrap(x):
    return lax.rem(x + 2 * CHIPS, CHIPS)


class Place:
    def __init__(self):
        self.seq = lax.axis_index("seq")
        self.n_seq = lax.axis_size("seq")
        me = lax.axis_index("nbr")
        self.me = me
        self.z = me // 2
        self.core = lax.rem(me, 2)
        self.d = 1 - 2 * self.core
        self.sibling = me + self.d

    def on(self, chip):
        return {"nbr": 2 * wrap(chip) + self.core}


class Gather:
    def __init__(self, place, buf, forward_sems, sibling_sems, recv_sems):
        self.p, self.buf = place, buf
        self.fs, self.ss, self.rs = forward_sems, sibling_sems, recv_sems
        self.sent = []

    def copy(self, slot, target, sem):
        return pltpu.make_async_remote_copy(
            src_ref=self.buf.at[slot],
            dst_ref=self.buf.at[slot],
            send_sem=sem,
            recv_sem=self.rs.at[slot],
            device_id=target,
            device_id_type=MESH,
        )

    def start(self, slot, target, sem):
        c = self.copy(slot, target, sem)
        c.start()
        self.sent.append(c)

    def slot(self, chip):
        return 2 * wrap(chip) + self.p.core

    def to_sibling(self, chip, i):
        self.start(self.slot(chip), {"nbr": self.p.sibling}, self.ss.at[i])

    def arrived(self, slot):
        self.copy(slot, {"nbr": self.p.sibling}, self.ss.at[0]).wait_recv()

    def own(self):
        z = self.p.z
        self.start(self.slot(z), self.p.on(z + 1), self.fs.at[0])
        self.start(self.slot(z), self.p.on(z - 1), self.fs.at[1])
        self.to_sibling(z, 0)

    def step(self, h):
        z, d = self.p.z, self.p.d
        if h < 3:
            for j, sign in enumerate((1, -1)):
                self.arrived(self.slot(z - sign * h))
                self.start(self.slot(z - sign * h), self.p.on(z + sign), self.fs.at[2 * h + j])
                self.to_sibling(z - sign * h, 2 * h - 1 + j)
        elif h == 3:
            self.arrived(self.slot(z - 3 * d))
            self.start(self.slot(z - 3 * d), self.p.on(z + d), self.fs.at[6])
            self.to_sibling(z - 3 * d, 5)
            self.arrived(self.slot(z + 3 * d))
            self.to_sibling(z + 3 * d, 6)
        else:
            self.arrived(self.slot(z + 4))
            self.to_sibling(z + 4, 7)

    def from_sibling(self, chip):
        self.arrived(2 * wrap(chip) + 1 - self.p.core)

    def drain(self):
        for c in self.sent:
            c.wait_send()


class Reduce:
    def __init__(self, place, part, from_sib, box, out, sems):
        self.p, self.part, self.from_sib, self.box, self.out = place, part, from_sib, box, out
        self.sib_send, self.sib_recv, self.send, self.recv = sems

    def sign(self, i):
        return jnp.where((i == 0) | (lax.rem(i, 2) == 1), self.p.d, -self.p.d)

    def dest(self, i):
        return wrap(self.p.z + self.sign(i) * (4 - (i + 1) // 2))

    def sib_copy(self, i):
        c = self.dest(i)
        return pltpu.make_async_remote_copy(
            src_ref=self.part.at[c, 1 - self.p.core],
            dst_ref=self.from_sib.at[c],
            send_sem=self.sib_send.at[c],
            recv_sem=self.sib_recv.at[c],
            device_id={"nbr": self.p.sibling},
            device_id_type=MESH,
        )

    def ring_copy(self, i, land):
        return pltpu.make_async_remote_copy(
            src_ref=self.out.at[i],
            dst_ref=self.box.at[land],
            send_sem=self.send.at[i],
            recv_sem=self.recv.at[land],
            device_id=self.p.on(self.p.z + self.sign(i)),
            device_id_type=MESH,
        )

    def chip_sum(self, i):
        c = self.dest(i)
        return self.part[c, self.p.core].astype(F32) + self.from_sib[c].astype(F32)

    def item(self, i):
        self.sib_copy(i).wait_recv()
        starts = (i == 0) | (i == 2)

        @pl.when(starts)
        def _():
            self.out[i] = self.chip_sum(i).astype(BF16)

        @pl.when(jnp.logical_not(starts))
        def _():
            self.ring_copy(i, i).wait_recv()
            self.out[i] = (self.chip_sum(i) + self.box[i].astype(F32)).astype(BF16)

        self.ring_copy(i, jnp.where(i == 0, 1, i + 2)).start()

    def run(self, make):
        def body(i, _):
            make(self.dest(i))
            self.sib_copy(i).start()

            @pl.when(i >= 1)
            def _():
                self.item(i - 1)

            return 0

        lax.fori_loop(0, CHIPS, body, 0)

    def total(self):
        self.sib_copy(7).wait_recv()
        self.ring_copy(0, 7).wait_recv()
        self.ring_copy(0, 8).wait_recv()
        return self.chip_sum(7) + self.box[7].astype(F32) + self.box[8].astype(F32)

    def drain(self):
        def body(i, _):
            self.ring_copy(i, jnp.where(i == 0, 1, i + 2)).wait_send()
            self.sib_copy(i).wait_send()
            return 0

        lax.fori_loop(0, CHIPS - 1, body, 0)
        self.sib_copy(7).wait_send()


def kernel(
    tok_in, nbr_in, table, counts, dec_in, wq_in, wo_in, gain, wkv_in, wout_in,
    out_ref, enc_ref,
    tok_all, nbr_all, nbr_raw, nbr32, wdec, wq, wo, wkv, wout,
    qpad, cond, encq, ppart, psib, pbox, pout, enc_all, att, opart, osib, obox, oout,
    hq, hq_got, ha, ha_got,
    load_sems, tok_f, tok_s, tok_r, nbr_f, nbr_s, nbr_r, enc_f, enc_s, enc_r,
    p0, p1, p2, p3, o0, o1, o2, o3, halo_sems,
):
    p = Place()
    z, core = p.z, p.core
    scale = 1.0 / HEAD_DIM**0.5
    heads = wq.shape[1] // HEAD_DIM
    width = wq.shape[1]

    loads = []
    for j, (src, dst) in enumerate(
        ((tok_in, tok_all.at[p.me]), (nbr_in, nbr_raw), (dec_in, wdec), (wq_in, wq), (wo_in, wo), (wkv_in, wkv), (wout_in, wout))
    ):
        c = pltpu.make_async_copy(src, dst, load_sems.at[j])
        c.start()
        loads.append(c)

    ahead = lax.rem(p.seq + 1, p.n_seq)
    behind = lax.rem(p.seq + p.n_seq - 1, p.n_seq)
    barrier = pltpu.get_barrier_semaphore()
    for who in (p.on(z + 1), p.on(z - 1), {"nbr": p.sibling}, {"seq": ahead}, {"seq": behind}):
        pl.semaphore_signal(barrier, inc=1, device_id=who, device_id_type=MESH)
    loads[1].wait()
    nbr32[...] = nbr_raw[...].astype(F32)
    for c in range(CHIPS):
        pair = [nbr32[lax.rem(table[c, k], nbr32.shape[0])] for k in range(2)]
        nbr_all[p.me, pl.ds(16 * c, 16), :] = jnp.concatenate(pair, axis=0).astype(BF16)
    loads[0].wait()
    pl.semaphore_wait(barrier, 5)

    tok = Gather(p, tok_all, tok_f, tok_s, tok_r)
    nbr = Gather(p, nbr_all, nbr_f, nbr_s, nbr_r)
    tok.own()
    tok.step(1)
    nbr.own()
    tok.step(2)
    nbr.step(1)
    tok.step(3)
    nbr.step(2)
    tok.step(4)
    for h in range(CHIPS):
        tok.from_sibling(z + h)
    loads[2].wait()

    def project(j):
        x = tok_all[...].reshape(16 * tok_all.shape[1], tok_all.shape[2])
        return dot(x, wdec[j])

    cond[0] = project(1).astype(BF16)
    nbr.step(3)
    cond[1] = project(2).astype(BF16)
    loads[3].wait()

    def enc_queries(chip):
        for k in range(2):
            n = 2 * wrap(chip) + k
            encq[n] = dot(nbr_all[n], wq[...]).astype(BF16)

    for h in (0, 1, -1, 2, -2):
        nbr.from_sibling(z + h)

    def early(i, _):
        enc_queries(z + i - 2)
        return 0

    lax.fori_loop(0, 5, early, 0)
    nbr.step(4)
    qpad[pl.ds(1, 512), :] = project(0).astype(BF16).astype(F32)
    hq[...] = qpad[pl.ds(0, GROUP), :].astype(BF16)

    def halo(src, dst, target, j):
        return pltpu.make_async_remote_copy(
            src_ref=src, dst_ref=dst, send_sem=halo_sems.at[2 * j], recv_sem=halo_sems.at[2 * j + 1],
            device_id={"seq": target}, device_id_type=MESH,
        )

    send_q = halo(hq, hq_got, behind, 0)
    send_q.start()
    for h in (3, -3, 4):
        nbr.from_sibling(z + h)

    def late(i, _):
        enc_queries(z + i + 3)
        return 0

    lax.fori_loop(0, 3, late, 0)
    loads[4].wait()

    def encode(c):
        queries = encq[:, pl.ds(pl.multiple_of(16 * c, 16), 16), :].reshape(2 * NLEN, width)
        mine = pl.ds(pl.multiple_of(GROUP * c, GROUP), GROUP)
        per_head = []
        for h in range(heads):
            cols = slice(HEAD_DIM * h, HEAD_DIM * (h + 1))
            weights = softmax(dot_t(queries[:, cols], cond[0, mine, cols]) * scale)
            per_head.append(dot(weights, cond[1, mine, cols]).astype(BF16))
        summed = dot(jnp.concatenate(per_head, axis=1), wo[...])
        summed = summed.reshape(16, 2, 8, summed.shape[1])
        for k in range(2):
            ppart[c, k] = summed[:, k].reshape(NLEN, summed.shape[3]).astype(BF16)

    enc_sum = Reduce(p, ppart, psib, pbox, pout, (p0, p1, p2, p3))
    enc_sum.run(encode)
    raw = nbr_all[:, pl.ds(pl.multiple_of(16 * z, 16), 16), :].astype(F32).reshape(16, 2, 8, -1)
    raw = jnp.where(core == 0, raw[:, 0], raw[:, 1]).reshape(NLEN, -1)
    combined = raw + enc_sum.total()
    factor = lax.rsqrt(jnp.mean(combined * combined, axis=-1, keepdims=True) + 1e-06)
    encoded = (combined * factor * gain[...]).astype(BF16)
    enc_all[p.me] = encoded
    enc = Gather(p, enc_all, enc_f, enc_s, enc_r)
    enc.own()
    enc_ref[...] = encoded
    loads[5].wait()
    loads[6].wait()
    send_q.wait_recv()

    def attend(g, last):
        rows = enc_all[pl.ds(2 * g, 2)].reshape(2 * NLEN, -1)
        keys = dot(rows, wkv[0]).astype(BF16)
        values = dot(rows, wkv[1]).astype(BF16)
        queries = qpad[pl.ds(pl.multiple_of(GROUP * (g + 1), GROUP), GROUP), :]
        first = lax.broadcasted_iota(jnp.int32, queries.shape, 0) == 0
        queries = jnp.where(first | jnp.logical_not(last), queries, hq_got[...].astype(F32)).astype(BF16)
        count = counts[p.seq * CHIPS + g]
        live = lax.broadcasted_iota(jnp.int32, (GROUP, 2 * NLEN), 1) < NLEN * count
        per_head = []
        for h in range(heads):
            cols = slice(HEAD_DIM * h, HEAD_DIM * (h + 1))
            scores = jnp.where(live, dot_t(queries[:, cols], keys[:, cols]) * scale, -1e30)
            per_head.append(dot(softmax(scores), values[:, cols]))
        got = jnp.concatenate(per_head, axis=1).astype(BF16)
        att[pl.ds(pl.multiple_of(GROUP * (g + 1), GROUP), GROUP), :] = got.astype(F32)

    def attend_all(first, count):
        def body(i, _):
            sign = jnp.where(lax.rem(i, 2) == 1, 1, -1)
            g = wrap(z + sign * ((i + 1) // 2))
            attend(g, g == CHIPS - 1)
            return 0

        lax.fori_loop(first, first + count, body, 0)

    enc.step(1)
    enc.from_sibling(z)
    attend_all(0, 1)
    enc.step(2)
    enc.from_sibling(z + 1)
    enc.from_sibling(z - 1)
    attend_all(1, 2)
    enc.step(3)
    enc.from_sibling(z + 2)
    enc.from_sibling(z - 2)
    attend_all(3, 2)
    enc.step(4)
    enc.from_sibling(z + 3)
    enc.from_sibling(z - 3)
    attend_all(5, 2)
    enc.from_sibling(z + 4)
    attend_all(7, 1)
    ha[...] = att[pl.ds(GROUP * CHIPS, GROUP), :].astype(BF16)
    send_a = halo(ha, ha_got, ahead, 1)
    send_a.start()
    send_a.wait_recv()
    begins = lax.rem(p.seq * (GROUP * CHIPS), SEQ_LEN) == 0
    att[pl.ds(0, GROUP), :] = jnp.where(begins, 0.0, ha_got[...].astype(F32))

    half = GROUP // 2
    block = 512

    def project_out(c):
        wide = att[pl.ds(pl.multiple_of(GROUP * c, GROUP), GROUP + 8), :]
        rows = wide[1 : GROUP + 1].astype(BF16)

        def body(j, _):
            cols = pl.ds(pl.multiple_of(j * block, block), block)
            y = dot(rows, wout[:, cols]).astype(BF16)
            opart[c, 0, :, cols] = y[:half]
            opart[c, 1, :, cols] = y[half:]
            return 0

        lax.fori_loop(0, wout.shape[1] // block, body, 0)

    out_sum = Reduce(p, opart, osib, obox, oout, (o0, o1, o2, o3))
    out_sum.run(project_out)
    out_ref[...] = out_sum.total().astype(BF16)

    for g in (tok, nbr, enc):
        g.drain()
    enc_sum.drain()
    out_sum.drain()
    send_q.wait_send()
    send_a.wait_send()


def local(
    tokens, nbr_embed, neighbour_table, valid_counts, dec_proj, enc_query, enc_out, enc_gain, nbr_proj, out_proj
):
    rows, model = tokens.shape
    nbrs, piece, enc_width = nbr_embed.shape
    width = enc_query.shape[1]
    chunk = nbrs * piece
    dma = pltpu.SemaphoreType.DMA
    scratch = [
        pltpu.VMEM((16, rows, model), BF16),
        pltpu.VMEM((16, chunk, enc_width), BF16),
        pltpu.VMEM((nbrs, piece, enc_width), BF16),
        pltpu.VMEM((nbrs, piece, enc_width), F32),
        pltpu.VMEM((3, model, width), BF16),
        pltpu.VMEM((enc_width, width), BF16),
        pltpu.VMEM((width, enc_width), BF16),
        pltpu.VMEM((2, enc_width, width), BF16),
        pltpu.VMEM((width, model), BF16),
        pltpu.VMEM((GROUP * (CHIPS + 1) + 8, width), F32),
        pltpu.VMEM((2, GROUP * CHIPS, width), BF16),
        pltpu.VMEM((16, chunk, width), BF16),
        pltpu.VMEM((CHIPS, 2, NLEN, enc_width), BF16),
        pltpu.VMEM((CHIPS, NLEN, enc_width), BF16),
        pltpu.VMEM((CHIPS + 1, NLEN, enc_width), BF16),
        pltpu.VMEM((CHIPS - 1, NLEN, enc_width), BF16),
        pltpu.VMEM((16, NLEN, enc_width), BF16),
        pltpu.VMEM((GROUP * (CHIPS + 1) + 8, width), F32),
        pltpu.VMEM((CHIPS, 2, rows, model), BF16),
        pltpu.VMEM((CHIPS, rows, model), BF16),
        pltpu.VMEM((CHIPS + 1, rows, model), BF16),
        pltpu.VMEM((CHIPS - 1, rows, model), BF16),
        *[pltpu.VMEM((GROUP, width), BF16)] * 4,
        dma((7,)),
        *[dma((7,)), dma((8,)), dma((16,))] * 3,
        *[dma((8,)), dma((8,)), dma((7,)), dma((9,))] * 2,
        dma((4,)),
    ]
    any_space = pl.BlockSpec(memory_space=pl.ANY)
    smem = pl.BlockSpec(memory_space=pltpu.SMEM)
    vmem = pl.BlockSpec(memory_space=pltpu.VMEM)
    return pl.pallas_call(
        kernel,
        out_shape=(
            jax.ShapeDtypeStruct((rows, model), BF16),
            jax.ShapeDtypeStruct((NLEN, enc_width), BF16),
        ),
        in_specs=[any_space, any_space, smem, smem, any_space, any_space, any_space, vmem, any_space, any_space],
        out_specs=(vmem, vmem),
        scratch_shapes=scratch,
        compiler_params=pltpu.CompilerParams(
            collective_id=0, has_side_effects=True, vmem_limit_bytes=60 * 2**20
        ),
        name="retrieval",
    )(
        tokens,
        nbr_embed,
        neighbour_table,
        valid_counts,
        jnp.transpose(dec_proj, (1, 0, 2)),
        enc_query,
        enc_out,
        enc_gain.reshape(1, enc_width),
        jnp.transpose(nbr_proj, (1, 0, 2)),
        out_proj,
    )


def solution(mesh):
    return jax.shard_map(
        local,
        mesh=mesh,
        in_specs=(
            P(("seq", "nbr"), None),
            P("seq", "nbr", None),
            P("seq", None),
            P(),
            P(None, None, "nbr"),
            P(None, "nbr"),
            P("nbr", None),
            P(),
            P(None, None, "nbr"),
            P("nbr", None),
        ),
        out_specs=(P(("seq", "nbr"), None), P(("seq", "nbr"), None)),
        check_vma=False,
    )
```

```python
import functools
import types

import jax
import jax.numpy as jnp
from jax import lax
from jax.experimental import pallas as pl
from jax.experimental.pallas import tpu as pltpu
from jax.sharding import PartitionSpec as P

HEAD_DIM = 128
GROUP = 64
NLEN = 128
SEQ_LEN = 2048
CHIPS = 8
F32 = jnp.float32
BF16 = jnp.bfloat16
MESH = pl.DeviceIdType.MESH


def dot(a, b):
    return jnp.dot(a, b, preferred_element_type=F32)


def dot_t(a, b):
    return lax.dot_general(a, b, (((1,), (1,)), ((), ())), preferred_element_type=F32)


def softmax(scores):
    peak = jnp.max(scores, axis=-1, keepdims=True)
    raised = jnp.exp(scores - peak)
    return (raised * (1.0 / jnp.sum(raised, axis=-1, keepdims=True))).astype(BF16)


def wrap(x):
    return lax.rem(x + 2 * CHIPS, CHIPS)


class Place:
    def __init__(self):
        self.seq = lax.axis_index("seq")
        self.n_seq = lax.axis_size("seq")
        me = lax.axis_index("nbr")
        self.me = me
        self.z = me // 2
        self.core = lax.rem(me, 2)
        self.d = 1 - 2 * self.core
        self.sibling = me + self.d

    def on(self, chip):
        return {"nbr": 2 * wrap(chip) + self.core}

    def nth(self, i):
        sign = jnp.where(lax.rem(i, 2) == 1, 1, -1)
        return wrap(self.z + sign * ((i + 1) // 2))


class Gather:
    def __init__(self, place, ref, forward_sems, recv_sems, sibling_sems=None):
        self.p, self.ref = place, ref
        self.fs, self.rs, self.ss = forward_sems, recv_sems, sibling_sems
        self.sent = []

    def copy(self, chip, core, target, sem):
        slot = 2 * wrap(chip) + core
        return pltpu.make_async_remote_copy(
            src_ref=self.ref(slot),
            dst_ref=self.ref(slot),
            send_sem=sem,
            recv_sem=self.rs.at[slot],
            device_id=target,
            device_id_type=MESH,
        )

    def start(self, chip, target, sem):
        c = self.copy(chip, self.p.core, target, sem)
        c.start()
        self.sent.append(c)

    def to_sibling(self, chip, i):
        if self.ss is not None:
            self.start(chip, {"nbr": self.p.sibling}, self.ss.at[i])

    def arrived(self, chip):
        self.copy(chip, self.p.core, {"nbr": self.p.sibling}, self.fs.at[0]).wait_recv()

    def from_sibling(self, chip):
        self.copy(chip, 1 - self.p.core, {"nbr": self.p.sibling}, self.fs.at[0]).wait_recv()

    def own(self):
        z = self.p.z
        self.start(z, self.p.on(z + 1), self.fs.at[0])
        self.start(z, self.p.on(z - 1), self.fs.at[1])
        self.to_sibling(z, 0)

    def step(self, h):
        z, d = self.p.z, self.p.d
        if h < 3:
            for j, sign in enumerate((1, -1)):
                self.arrived(z - sign * h)
                self.start(z - sign * h, self.p.on(z + sign), self.fs.at[2 * h + j])
                self.to_sibling(z - sign * h, 2 * h - 1 + j)
        elif h == 3:
            self.arrived(z - 3 * d)
            self.start(z - 3 * d, self.p.on(z + d), self.fs.at[6])
            self.to_sibling(z - 3 * d, 5)
            self.arrived(z + 3 * d)
            self.to_sibling(z + 3 * d, 6)
        else:
            self.arrived(z + 4)
            self.to_sibling(z + 4, 7)

    def drain(self):
        for c in self.sent:
            c.wait_send()


class Spread:
    def __init__(self, place, piece, slab, first, second, sems):
        self.p, self.piece, self.slab = place, piece, slab
        (self.a, self.to_first), (self.b, self.to_second) = first, second
        self.bs, self.br, self.cs, self.cr, self.ds, self.dr, self.es, self.er = sems
        self.sent = []

    def copy(self, ref, target, send, recv):
        return pltpu.make_async_remote_copy(
            src_ref=ref, dst_ref=ref, send_sem=send, recv_sem=recv, device_id=target, device_id_type=MESH
        )

    def start(self, *copy):
        c = self.copy(*copy)
        c.start()
        self.sent.append(c)

    def send_both(self, i, ref, to, send, recv):
        for j, sign in enumerate((1, -1)):
            self.start(ref, to(sign), send.at[i, j], recv.at[i, j])

    def pass_on(self, i, ref, to, arrived, send, recv):
        for j, sign in enumerate((1, -1)):
            self.copy(ref(-sign), to(sign), send.at[i], arrived.at[i, j]).wait_recv()
        sign = 1 if i % 2 else -1
        self.start(ref(-sign), to(sign), send.at[i], recv.at[i])

    def piece_at(self, i, shift):
        return self.piece(self.p.nth(i), lax.rem(self.a + shift + 4, 4))

    def slab_at(self, i, shift):
        return self.slab(self.p.nth(i), lax.rem(self.b + shift + 4, 4))

    def pieces_out(self, i):
        self.send_both(i, self.piece_at(i, 0), self.to_first, self.bs, self.br)

    def pieces_on(self, i):
        self.pass_on(i, functools.partial(self.piece_at, i), self.to_first, self.br, self.cs, self.cr)

    def slabs_out(self, i):
        self.copy(self.piece_at(i, 2), self.to_first(1), self.cs.at[i], self.cr.at[i]).wait_recv()
        self.send_both(i, self.slab_at(i, 0), self.to_second, self.ds, self.dr)

    def slabs_on(self, i):
        self.pass_on(i, functools.partial(self.slab_at, i), self.to_second, self.dr, self.es, self.er)

    def ready(self, i):
        self.copy(self.slab_at(i, 2), self.to_second(1), self.es.at[i], self.er.at[i]).wait_recv()

    def drain(self):
        for c in self.sent:
            c.wait_send()


class Reduce:
    def __init__(self, place, part, from_sib, box, out, sems):
        self.p, self.part, self.from_sib, self.box, self.out = place, part, from_sib, box, out
        self.sib_send, self.sib_recv, self.send, self.recv = sems

    def sign(self, i):
        return jnp.where((i == 0) | (lax.rem(i, 2) == 1), self.p.d, -self.p.d)

    def dest(self, i):
        return wrap(self.p.z + self.sign(i) * (4 - (i + 1) // 2))

    def sib_copy(self, k, c):
        return pltpu.make_async_remote_copy(
            src_ref=self.part.at[k, c, 1 - self.p.core],
            dst_ref=self.from_sib.at[k, c],
            send_sem=self.sib_send.at[k, c],
            recv_sem=self.sib_recv.at[k, c],
            device_id={"nbr": self.p.sibling},
            device_id_type=MESH,
        )

    def ring_copy(self, k, i, land):
        return pltpu.make_async_remote_copy(
            src_ref=self.out.at[k, i],
            dst_ref=self.box.at[k, land],
            send_sem=self.send.at[k, i],
            recv_sem=self.recv.at[k, land],
            device_id=self.p.on(self.p.z + self.sign(i)),
            device_id_type=MESH,
        )

    def chip_sum(self, k, i):
        c = self.dest(i)
        return self.part[k, c, self.p.core].astype(F32) + self.from_sib[k, c].astype(F32)

    def item(self, k, i):
        self.sib_copy(k, self.dest(i)).wait_recv()
        starts = (i == 0) | (i == 2)

        @pl.when(starts)
        def _():
            self.out[k, i] = self.chip_sum(k, i).astype(BF16)

        @pl.when(jnp.logical_not(starts))
        def _():
            self.ring_copy(k, i, i).wait_recv()
            self.out[k, i] = (self.chip_sum(k, i) + self.box[k, i].astype(F32)).astype(BF16)

        self.ring_copy(k, i, jnp.where(i == 0, 1, i + 2)).start()

    def total(self, k):
        self.sib_copy(k, self.p.z).wait_recv()
        self.ring_copy(k, 0, 7).wait_recv()
        self.ring_copy(k, 0, 8).wait_recv()
        return self.chip_sum(k, jnp.int32(7)) + self.box[k, 7].astype(F32) + self.box[k, 8].astype(F32)

    def drain(self):
        def body(i, _):
            for k in range(2):
                self.ring_copy(k, i, i).wait_send()
                self.sib_copy(k, i).wait_send()
            return 0

        lax.fori_loop(0, CHIPS - 1, body, 0)
        for k in range(2):
            self.sib_copy(k, CHIPS - 1).wait_send()


def kernel(names, *refs):
    r = types.SimpleNamespace(**dict(zip(names, refs, strict=True)))
    p = Place()
    z, core = p.z, p.core
    scale = 1.0 / HEAD_DIM**0.5
    width = r.wkv.shape[2]
    heads = width // HEAD_DIM
    model = r.wout.shape[1]
    enc_width = r.wkv.shape[1]
    half_model = model // 2
    half_rows = NLEN // 2
    x, y = p.seq // 4, lax.rem(p.seq, 4)

    loads = []
    for j, (src, dst) in enumerate(
        (
            (r.nbr_in, r.nbr_raw),
            (r.wq_in, r.wq_all.at[z]),
            (r.wo_in, r.wo_all.at[z]),
            (r.tok_in.at[:, pl.ds(0, half_model)], r.tok_all.at[0, p.me]),
            (r.tok_in.at[:, pl.ds(half_model, half_model)], r.tok_all.at[1, p.me]),
            (r.dec_in, r.wdec),
            (r.wkv_in, r.wkv_raw),
            (r.wout_in, r.wout),
        )
    ):
        c = pltpu.make_async_copy(src, dst, r.load_sems.at[j])
        c.start()
        loads.append(c)
    load_nbr, load_q, load_o, load_tok0, load_tok1, load_dec, load_kv, load_out = loads

    def to_x(shift):
        return {"seq": 4 * lax.rem(x + shift + 4, 4) + y}

    def to_y(shift):
        return {"seq": 4 * x + lax.rem(y + shift + 4, 4)}

    ahead = lax.rem(p.seq + 1, p.n_seq)
    behind = lax.rem(p.seq + p.n_seq - 1, p.n_seq)
    partners = [p.on(z + h) for h in range(1, CHIPS)]
    partners += [{"nbr": p.sibling}, to_x(1), to_x(-1), to_y(1), to_y(-1), {"seq": ahead}, {"seq": behind}]
    barrier = pltpu.get_barrier_semaphore()
    for who in partners:
        pl.semaphore_signal(barrier, inc=1, device_id=who, device_id_type=MESH)
    load_nbr.wait()
    r.nbr32[...] = r.nbr_raw[...].astype(F32)
    for c in range(CHIPS):
        pair = [r.nbr32[lax.rem(r.table[k, c], r.nbr32.shape[0])] for k in range(2)]
        r.nbr_send[c] = jnp.concatenate(pair, axis=0).astype(BF16)
    r.nbr_all[z, core] = r.nbr_send[z]
    for c in (load_q, load_o, load_tok0, load_tok1):
        c.wait()
    pl.semaphore_wait(barrier, len(partners))

    def query_piece(chip, a):
        rows = pl.ds(pl.multiple_of(224 * y + 112 * (a // 2), 16), 112)
        return r.wq_all.at[chip, rows, pl.ds(pl.multiple_of(128 * lax.rem(a, 2), 128), 128)]

    def query_slab(chip, b):
        return r.wq_all.at[chip, pl.ds(pl.multiple_of(224 * b, 16), 224)]

    def out_piece(chip, a):
        return r.wo_all.at[chip, pl.ds(pl.multiple_of(64 * x + 16 * a, 16), 16)]

    def out_slab(chip, b):
        return r.wo_all.at[chip, pl.ds(pl.multiple_of(64 * b, 16), 64)]

    def stream(name, k, ref, sibling=True):
        sems = [getattr(r, name + end).at[k] for end in ("_f", "_r", "_s")[: 2 + sibling]]
        return Gather(p, ref, *sems)

    tok, enc = ([stream(name, k, getattr(r, name + "_all").at[k].at.__getitem__) for k in range(2)] for name in ("tok", "enc"))
    weights_z = [
        stream("wz", 0, lambda slot: query_piece(slot // 2, x), False),
        stream("wz", 1, lambda slot: out_piece(slot // 2, y), False),
    ]
    spread_sems = [getattr(r, "x" + c) for c in "abcdefgh"]
    weights_xy = [
        Spread(p, query_piece, query_slab, (x, to_x), (y, to_y), [s.at[0] for s in spread_sems]),
        Spread(p, out_piece, out_slab, (y, to_y), (x, to_x), [s.at[1] for s in spread_sems]),
    ]

    def weights(what, *items):
        for i in items:
            for w in weights_xy:
                getattr(w, what)(i)

    def weights_step(h):
        for w in weights_z:
            w.step(h)

    def remote(src, dst, target, send, recv):
        return pltpu.make_async_remote_copy(
            src_ref=src, dst_ref=dst, send_sem=send, recv_sem=recv, device_id=target, device_id_type=MESH
        )

    def halo(src, dst, target, j):
        return remote(src, dst, {"seq": target}, r.halo_sems.at[2 * j], r.halo_sems.at[2 * j + 1])

    send_q = halo(r.hq, r.hq_got, behind, 0)
    send_a = halo(r.ha, r.ha_got, ahead, 1)

    def nbr_copy(h):
        return remote(
            r.nbr_send.at[wrap(z + h)], r.nbr_all.at[z, core], p.on(z + h), r.nbr_sems.at[0, h], r.nbr_sems.at[1, z]
        )

    def nbr_arrived(h):
        chip = wrap(z + h)
        remote(
            r.nbr_send.at[0], r.nbr_all.at[chip, core], p.on(chip), r.nbr_sems.at[0, 0], r.nbr_sems.at[1, chip]
        ).wait_recv()

    nbr_sib = remote(
        r.nbr_all.at[:, core], r.nbr_all.at[:, core], {"nbr": p.sibling}, r.pair_sems.at[0], r.pair_sems.at[1]
    )
    nbr_sib_in = remote(
        r.nbr_all.at[:, 1 - core], r.nbr_all.at[:, 1 - core], {"nbr": p.sibling}, r.pair_sems.at[0], r.pair_sems.at[1]
    )

    def cond_copy(j, h):
        mine = pl.ds(pl.multiple_of(GROUP * wrap(z + h), GROUP), GROUP)
        return remote(
            r.cond.at[j, mine], r.cond_got.at[z, j], p.on(z + h), r.cond_s.at[j, h], r.cond_r.at[j, z]
        )

    def cond_arrived(j, chip):
        remote(
            r.cond.at[j, pl.ds(0, GROUP)], r.cond_got.at[chip, j], p.on(chip), r.cond_s.at[j, 0], r.cond_r.at[j, chip]
        ).wait_recv()

    order = (1, -1, 2, -2, 3, -3, 4)

    def project(j):
        x0, x1 = (r.tok_all[k].reshape(CHIPS * GROUP, half_model) for k in range(2))
        return dot(x0, r.wdec[j, pl.ds(0, half_model)]) + dot(x1, r.wdec[j, pl.ds(half_model, half_model)])

    def make_cond(j):
        r.cond[j] = project(1 + j).astype(BF16)
        for h in order:
            cond_copy(j, h % CHIPS).start()
        r.cond_got[z, j] = r.cond[j, pl.ds(pl.multiple_of(GROUP * z, GROUP), GROUP)]

    def encode(i, _):
        chip = p.nth(i)

        @pl.when(i >= 1)
        def _():
            for j in range(2):
                cond_arrived(j, chip)
            for w in weights_xy:
                w.ready(i)

        queries = dot(r.nbr_all[...].reshape(2 * NLEN, enc_width), r.wq_all[chip]).astype(BF16)
        per_head = []
        for h in range(heads):
            cols = slice(HEAD_DIM * h, HEAD_DIM * (h + 1))
            shares = softmax(dot_t(queries[:, cols], r.cond_got[chip, 0, :, cols]) * scale)
            per_head.append(dot(shares, r.cond_got[chip, 1, :, cols]).astype(BF16))
        term = dot(jnp.concatenate(per_head, axis=1), r.wo_all[chip])

        @pl.when(i == 0)
        def _():
            r.enc_sum[...] = term

        @pl.when(i >= 1)
        def _():
            r.enc_sum[...] += term

        return 0

    def of_slot(rows, slot):
        rows = rows.reshape(16, 2, 8, enc_width)
        return jnp.where(slot == 0, rows[:, 0], rows[:, 1]).reshape(NLEN, enc_width)

    sum_copy = remote(r.sum_out, r.sum_got, {"nbr": p.sibling}, r.pair_sems.at[2], r.pair_sems.at[3])

    def split_kv():
        step = 128

        def body(i, _):
            mine = pl.ds(pl.multiple_of(i * step, step), step)
            both = r.wkv_raw[mine].astype(F32)
            r.wkv[0, mine] = both[:, 0].astype(BF16)
            r.wkv[1, mine] = both[:, 1].astype(BF16)
            return 0

        lax.fori_loop(0, enc_width // step, body, 0)

    def make_kv(k, g):
        rows = r.enc_all[k, pl.ds(2 * g, 2)].reshape(NLEN, enc_width)
        for j in range(2):
            r.kv[j, g, pl.ds(NLEN * k, NLEN)] = dot(rows, r.wkv[j]).astype(BF16)

    def attend(g):
        queries = r.qpad[pl.ds(pl.multiple_of(GROUP * (g + 1), GROUP), GROUP), :]
        own = (lax.broadcasted_iota(jnp.int32, queries.shape, 0) == 0) | (g != CHIPS - 1)
        queries = jnp.where(own, queries, r.hq_got[...].astype(F32)).astype(BF16)
        count = r.counts[p.seq * CHIPS + g]
        key = lax.broadcasted_iota(jnp.int32, (GROUP, 2 * NLEN), 1)
        live = lax.rem(key // half_rows, 2) < count
        per_head = []
        for h in range(heads):
            cols = slice(HEAD_DIM * h, HEAD_DIM * (h + 1))
            scores = jnp.where(live, dot_t(queries[:, cols], r.kv[0, g, :, cols]) * scale, -1e30)
            per_head.append(dot(softmax(scores), r.kv[1, g, :, cols]))
        got = jnp.concatenate(per_head, axis=1).astype(BF16)
        r.att[pl.ds(pl.multiple_of(GROUP * (g + 1), GROUP), GROUP), :] = got.astype(F32)

        @pl.when(g == CHIPS - 1)
        def _():
            r.ha[...] = got
            send_a.start()

    def attend_all(first, count):
        def body(i, _):
            make_kv(1, p.nth(i))
            attend(p.nth(i))
            return 0

        lax.fori_loop(first, first + count, body, 0)

    out_sum = Reduce(p, r.opart, r.osib, r.obox, r.oout, (r.o0, r.o1, r.o2, r.o3))
    half = GROUP // 2
    block = 512

    def make_out(c):
        @pl.when(c == 0)
        def _():
            send_a.wait_recv()
            begins = lax.rem(p.seq * (GROUP * CHIPS), SEQ_LEN) == 0
            r.att[pl.ds(0, GROUP), :] = jnp.where(begins, 0.0, r.ha_got[...].astype(F32))

        wide = r.att[pl.ds(pl.multiple_of(GROUP * c, GROUP), GROUP + 8), :]
        rows = wide[1 : GROUP + 1].astype(BF16)

        for k in range(2):

            def body(j, _, k=k):
                cols = pl.ds(pl.multiple_of(j * block, block), block)
                weight = r.wout[:, pl.ds(pl.multiple_of(k * half_model + j * block, block), block)]
                y = dot(rows, weight).astype(BF16)
                r.opart[k, c, 0, :, cols] = y[:half]
                r.opart[k, c, 1, :, cols] = y[half:]
                return 0

            lax.fori_loop(0, half_model // block, body, 0)
            out_sum.sib_copy(k, c).start()

    def make_outs(chips):
        for c in chips:
            make_out(wrap(c))

    for g in (*weights_z, *tok):
        g.own()
    load_kv.wait()
    split_kv()
    weights_step(1)
    weights("pieces_out", 1, 2)
    tok[0].step(1)
    weights("pieces_on", 1, 2)
    tok[1].step(1)
    weights_step(2)
    weights("slabs_out", 1, 2)
    weights("pieces_out", 3, 4)
    tok[0].step(2)
    weights("pieces_on", 3, 4)
    weights("slabs_on", 1)
    tok[1].step(2)
    weights_step(3)
    weights("slabs_on", 2)
    weights("slabs_out", 3, 4)
    weights("pieces_out", 5, 6)
    tok[0].step(3)
    weights("pieces_on", 5, 6)
    weights("slabs_on", 3)
    tok[1].step(3)
    for h in order:
        nbr_copy(h % CHIPS).start()
    weights_step(4)
    weights("slabs_on", 4)
    weights("slabs_out", 5, 6)
    weights("pieces_out", 7)
    tok[0].step(4)
    weights("pieces_on", 7)
    tok[1].step(4)
    for t in tok:
        for h in range(CHIPS):
            t.from_sibling(z + h)
    weights("slabs_out", 7)
    load_dec.wait()
    make_cond(0)
    weights("slabs_on", 5)
    make_cond(1)
    weights("slabs_on", 6)
    r.qpad[pl.ds(1, CHIPS * GROUP), :] = project(0).astype(BF16).astype(F32)
    r.hq[...] = r.qpad[pl.ds(0, GROUP), :].astype(BF16)
    send_q.start()
    weights("slabs_on", 7)
    for h in order:
        nbr_arrived(h)
    nbr_sib.start()
    nbr_sib_in.wait_recv()
    lax.fori_loop(0, CHIPS, encode, 0)

    r.sum_out[...] = of_slot(r.enc_sum[...], 1 - core).astype(BF16)
    sum_copy.start()
    raw = of_slot(r.nbr_all[...].astype(F32).reshape(2 * NLEN, enc_width), core)
    mine = raw + of_slot(r.enc_sum[...], core)
    sum_copy.wait_recv()
    combined = mine + r.sum_got[...].astype(F32)
    factor = lax.rsqrt(jnp.mean(combined * combined, axis=-1, keepdims=True) + 1e-06)
    encoded = (combined * factor * r.gain[...].reshape(1, enc_width)).astype(BF16)
    for k in range(2):
        r.enc_all[k, p.me] = encoded[half_rows * k : half_rows * (k + 1)]
        enc[k].own()
    r.enc_ref[...] = encoded
    send_q.wait_recv()
    load_out.wait()
    for h in (1, 2):
        for k in range(2):
            enc[k].step(h)
    for h in (0, 1, -1, 2, -2):
        enc[0].from_sibling(z + h)

    def first_kv(i, _):
        make_kv(0, p.nth(i))
        return 0

    lax.fori_loop(0, 5, first_kv, 0)
    for h in (0, 1, -1):
        enc[1].from_sibling(z + h)
    attend_all(0, 3)
    enc[0].step(3)
    enc[1].step(3)
    make_outs((z, z + 1))
    for h in (2, -2):
        enc[1].from_sibling(z + h)
    attend_all(3, 2)
    enc[0].step(4)
    enc[1].step(4)
    make_outs((z - 1, z + 2))
    for h in (3, -3, 4):
        enc[0].from_sibling(z + h)
    lax.fori_loop(5, CHIPS, first_kv, 0)
    for h in (3, -3):
        enc[1].from_sibling(z + h)
    attend_all(5, 2)
    enc[1].from_sibling(z + 4)
    attend_all(7, 1)
    make_outs((z + 4,))
    for k in range(2):
        out_sum.item(k, jnp.int32(0))
    make_outs((z - 3, z + 3, z - 2))

    def out_items(i, _):
        for k in range(2):
            out_sum.item(k, i)
        return 0

    lax.fori_loop(1, CHIPS - 1, out_items, 0)
    for k in range(2):
        r.out_ref[:, pl.ds(k * half_model, half_model)] = out_sum.total(k).astype(BF16)

    for g in (*tok, *enc, *weights_z, *weights_xy):
        g.drain()
    out_sum.drain()
    for h in range(1, CHIPS):
        nbr_copy(h).wait_send()
        for j in range(2):
            cond_copy(j, h).wait_send()
    for c in (nbr_sib, sum_copy, send_q, send_a):
        c.wait_send()


def local(
    tokens, nbr_embed, neighbour_table, valid_counts, dec_proj, enc_query, enc_out, enc_gain, nbr_proj, out_proj
):
    rows, model = tokens.shape
    nbrs, piece, enc_width = nbr_embed.shape
    width = enc_query.shape[1]
    block = 2 * piece
    sub = NLEN // 2
    padded = GROUP * (CHIPS + 1) + 8
    dma = pltpu.SemaphoreType.DMA
    half = (rows, model // 2)
    scratch = {
        "tok_all": pltpu.VMEM((2, 16, *half), BF16),
        "enc_all": pltpu.VMEM((2, 16, sub, enc_width), BF16),
        "nbr_all": pltpu.VMEM((CHIPS, 2, block, enc_width), BF16),
        "nbr_send": pltpu.VMEM((CHIPS, block, enc_width), BF16),
        "nbr_raw": pltpu.VMEM((nbrs, piece, enc_width), BF16),
        "nbr32": pltpu.VMEM((nbrs, piece, enc_width), F32),
        "wdec": pltpu.VMEM((3, model, width), BF16),
        "wq_all": pltpu.VMEM((CHIPS, enc_width, width), BF16),
        "wo_all": pltpu.VMEM((CHIPS, width, enc_width), BF16),
        "wkv_raw": pltpu.VMEM((enc_width, 2, width), BF16),
        "wkv": pltpu.VMEM((2, enc_width, width), BF16),
        "wout": pltpu.VMEM((width, model), BF16),
        "qpad": pltpu.VMEM((padded, width), F32),
        "cond": pltpu.VMEM((2, GROUP * CHIPS, width), BF16),
        "cond_got": pltpu.VMEM((CHIPS, 2, GROUP, width), BF16),
        "enc_sum": pltpu.VMEM((2 * NLEN, enc_width), F32),
        "sum_out": pltpu.VMEM((NLEN, enc_width), BF16),
        "sum_got": pltpu.VMEM((NLEN, enc_width), BF16),
        "kv": pltpu.VMEM((2, CHIPS, 2 * NLEN, width), BF16),
        "att": pltpu.VMEM((padded, width), F32),
        "opart": pltpu.VMEM((2, CHIPS, 2, *half), BF16),
        "osib": pltpu.VMEM((2, CHIPS, *half), BF16),
        "obox": pltpu.VMEM((2, CHIPS + 1, *half), BF16),
        "oout": pltpu.VMEM((2, CHIPS - 1, *half), BF16),
        **{name: pltpu.VMEM((GROUP, width), BF16) for name in ("hq", "hq_got", "ha", "ha_got")},
        "load_sems": dma((8,)),
        "halo_sems": dma((4,)),
        "nbr_sems": dma((2, CHIPS)),
        "pair_sems": dma((4,)),
        "cond_s": dma((2, CHIPS)),
        "cond_r": dma((2, CHIPS)),
        **{f"{name}_{x}": dma((2, n)) for name in ("tok", "enc", "wz") for x, n in (("f", 7), ("s", 8), ("r", 16))},
        **{f"x{c}": dma((2, CHIPS, 2)) if c in "abef" else dma((2, CHIPS)) for c in "abcdefgh"},
        **{f"o{j}": dma((2, n)) for j, n in enumerate((8, 8, 7, 9))},
    }
    inputs = {
        "tok_in": (tokens, pl.ANY),
        "nbr_in": (nbr_embed, pl.ANY),
        "table": (neighbour_table.T, pltpu.SMEM),
        "counts": (valid_counts, pltpu.SMEM),
        "dec_in": (jnp.transpose(dec_proj, (1, 0, 2)), pl.ANY),
        "wq_in": (enc_query, pl.ANY),
        "wo_in": (enc_out, pl.ANY),
        "gain": (enc_gain, pltpu.VMEM),
        "wkv_in": (nbr_proj, pl.ANY),
        "wout_in": (out_proj, pl.ANY),
    }
    vmem = pl.BlockSpec(memory_space=pltpu.VMEM)
    names = (*inputs, "out_ref", "enc_ref", *scratch)
    return pl.pallas_call(
        functools.partial(kernel, names),
        out_shape=(
            jax.ShapeDtypeStruct((rows, model), BF16),
            jax.ShapeDtypeStruct((NLEN, enc_width), BF16),
        ),
        in_specs=[pl.BlockSpec(memory_space=space) for _, space in inputs.values()],
        out_specs=(vmem, vmem),
        scratch_shapes=list(scratch.values()),
        compiler_params=pltpu.CompilerParams(
            collective_id=0, has_side_effects=True, vmem_limit_bytes=60 * 2**20
        ),
        name="retrieval",
    )(*(array for array, _ in inputs.values()))


def solution(mesh):
    return jax.shard_map(
        local,
        mesh=mesh,
        in_specs=(
            P(("seq", "nbr"), None),
            P("seq", "nbr", None),
            P("seq", None),
            P(),
            P(None, None, "nbr"),
            P(None, "nbr"),
            P("nbr", None),
            P(),
            P(None, None, "nbr"),
            P("nbr", None),
        ),
        out_specs=(P(("seq", "nbr"), None), P(("seq", "nbr"), None)),
        check_vma=False,
    )
```

```python
import functools
import types

import jax
import jax.numpy as jnp
from jax import lax
from jax.experimental import pallas as pl
from jax.experimental.pallas import tpu as pltpu
from jax.sharding import PartitionSpec as P

HEAD_DIM = 128
GROUP = 64
NLEN = 128
SEQ_LEN = 2048
CHIPS = 8
F32 = jnp.float32
BF16 = jnp.bfloat16
MESH = pl.DeviceIdType.MESH


def dot(a, b):
    return jnp.dot(a, b, preferred_element_type=F32)


def dot_t(a, b):
    return lax.dot_general(a, b, (((1,), (1,)), ((), ())), preferred_element_type=F32)


def softmax(scores):
    peak = jnp.max(scores, axis=-1, keepdims=True)
    raised = jnp.exp(scores - peak)
    return (raised * (1.0 / jnp.sum(raised, axis=-1, keepdims=True))).astype(BF16)


def wrap(x):
    return lax.rem(x + 2 * CHIPS, CHIPS)


class Place:
    def __init__(self):
        self.seq = lax.axis_index("seq")
        self.n_seq = lax.axis_size("seq")
        me = lax.axis_index("nbr")
        self.me = me
        self.z = me // 2
        self.core = lax.rem(me, 2)
        self.d = 1 - 2 * self.core
        self.sibling = me + self.d

    def on(self, chip):
        return {"nbr": 2 * wrap(chip) + self.core}

    def nth(self, i):
        sign = jnp.where(lax.rem(i, 2) == 1, 1, -1)
        return wrap(self.z + sign * ((i + 1) // 2))


class Gather:
    def __init__(self, place, ref, forward_sems, recv_sems, sibling_sems=None):
        self.p, self.ref = place, ref
        self.fs, self.rs, self.ss = forward_sems, recv_sems, sibling_sems
        self.sent = []

    def copy(self, chip, core, target, sem):
        slot = 2 * wrap(chip) + core
        return pltpu.make_async_remote_copy(
            src_ref=self.ref(slot),
            dst_ref=self.ref(slot),
            send_sem=sem,
            recv_sem=self.rs.at[slot],
            device_id=target,
            device_id_type=MESH,
        )

    def start(self, chip, target, sem):
        c = self.copy(chip, self.p.core, target, sem)
        c.start()
        self.sent.append(c)

    def to_sibling(self, chip, i):
        if self.ss is not None:
            self.start(chip, {"nbr": self.p.sibling}, self.ss.at[i])

    def arrived(self, chip):
        self.copy(chip, self.p.core, {"nbr": self.p.sibling}, self.fs.at[0]).wait_recv()

    def from_sibling(self, chip):
        self.copy(chip, 1 - self.p.core, {"nbr": self.p.sibling}, self.fs.at[0]).wait_recv()

    def own(self):
        z = self.p.z
        self.start(z, self.p.on(z + 1), self.fs.at[0])
        self.start(z, self.p.on(z - 1), self.fs.at[1])
        self.to_sibling(z, 0)

    def step(self, h):
        z, d = self.p.z, self.p.d
        if h < 3:
            for j, sign in enumerate((1, -1)):
                self.arrived(z - sign * h)
                self.start(z - sign * h, self.p.on(z + sign), self.fs.at[2 * h + j])
                self.to_sibling(z - sign * h, 2 * h - 1 + j)
        elif h == 3:
            self.arrived(z - 3 * d)
            self.start(z - 3 * d, self.p.on(z + d), self.fs.at[6])
            self.to_sibling(z - 3 * d, 5)
            self.arrived(z + 3 * d)
            self.to_sibling(z + 3 * d, 6)
        else:
            self.arrived(z + 4)
            self.to_sibling(z + 4, 7)

    def drain(self):
        for c in self.sent:
            c.wait_send()


class Spread:
    def __init__(self, place, piece, slab, first, second, sems):
        self.p, self.piece, self.slab = place, piece, slab
        (self.a, self.to_first), (self.b, self.to_second) = first, second
        self.bs, self.br, self.cs, self.cr, self.ds, self.dr, self.es, self.er = sems
        self.sent = []

    def copy(self, ref, target, send, recv):
        return pltpu.make_async_remote_copy(
            src_ref=ref, dst_ref=ref, send_sem=send, recv_sem=recv, device_id=target, device_id_type=MESH
        )

    def start(self, *copy):
        c = self.copy(*copy)
        c.start()
        self.sent.append(c)

    def send_both(self, i, ref, to, send, recv):
        for j, sign in enumerate((1, -1)):
            self.start(ref, to(sign), send.at[i, j], recv.at[i, j])

    def pass_on(self, i, ref, to, arrived, send, recv):
        for j, sign in enumerate((1, -1)):
            self.copy(ref(-sign), to(sign), send.at[i], arrived.at[i, j]).wait_recv()
        sign = 1 if i % 2 else -1
        self.start(ref(-sign), to(sign), send.at[i], recv.at[i])

    def piece_at(self, i, shift):
        return self.piece(self.p.nth(i), lax.rem(self.a + shift + 4, 4))

    def slab_at(self, i, shift):
        return self.slab(self.p.nth(i), lax.rem(self.b + shift + 4, 4))

    def pieces_out(self, i):
        self.send_both(i, self.piece_at(i, 0), self.to_first, self.bs, self.br)

    def pieces_on(self, i):
        self.pass_on(i, functools.partial(self.piece_at, i), self.to_first, self.br, self.cs, self.cr)

    def slabs_out(self, i):
        self.copy(self.piece_at(i, 2), self.to_first(1), self.cs.at[i], self.cr.at[i]).wait_recv()
        self.send_both(i, self.slab_at(i, 0), self.to_second, self.ds, self.dr)

    def slabs_on(self, i):
        self.pass_on(i, functools.partial(self.slab_at, i), self.to_second, self.dr, self.es, self.er)

    def ready(self, i):
        self.copy(self.slab_at(i, 2), self.to_second(1), self.es.at[i], self.er.at[i]).wait_recv()

    def drain(self):
        for c in self.sent:
            c.wait_send()


class Reduce:
    def __init__(self, place, part, from_sib, box, out, sems):
        self.p, self.part, self.from_sib, self.box, self.out = place, part, from_sib, box, out
        self.sib_send, self.sib_recv, self.send, self.recv = sems

    def sign(self, i):
        return jnp.where((i == 0) | (lax.rem(i, 2) == 1), self.p.d, -self.p.d)

    def dest(self, i):
        return wrap(self.p.z + self.sign(i) * (4 - (i + 1) // 2))

    def sib_copy(self, k, c):
        return pltpu.make_async_remote_copy(
            src_ref=self.part.at[k, c, 1 - self.p.core],
            dst_ref=self.from_sib.at[k, c],
            send_sem=self.sib_send.at[k, c],
            recv_sem=self.sib_recv.at[k, c],
            device_id={"nbr": self.p.sibling},
            device_id_type=MESH,
        )

    def ring_copy(self, k, i, land):
        return pltpu.make_async_remote_copy(
            src_ref=self.out.at[k, i],
            dst_ref=self.box.at[k, land],
            send_sem=self.send.at[k, i],
            recv_sem=self.recv.at[k, land],
            device_id=self.p.on(self.p.z + self.sign(i)),
            device_id_type=MESH,
        )

    def chip_sum(self, k, i):
        c = self.dest(i)
        return self.part[k, c, self.p.core].astype(F32) + self.from_sib[k, c].astype(F32)

    def item(self, k, i):
        self.sib_copy(k, self.dest(i)).wait_recv()
        starts = (i == 0) | (i == 2)

        @pl.when(starts)
        def _():
            self.out[k, i] = self.chip_sum(k, i).astype(BF16)

        @pl.when(jnp.logical_not(starts))
        def _():
            self.ring_copy(k, i, i).wait_recv()
            self.out[k, i] = (self.chip_sum(k, i) + self.box[k, i].astype(F32)).astype(BF16)

        self.ring_copy(k, i, jnp.where(i == 0, 1, i + 2)).start()

    def total(self, k):
        self.sib_copy(k, self.p.z).wait_recv()
        self.ring_copy(k, 0, 7).wait_recv()
        self.ring_copy(k, 0, 8).wait_recv()
        return self.chip_sum(k, jnp.int32(7)) + self.box[k, 7].astype(F32) + self.box[k, 8].astype(F32)

    def drain(self):
        def body(i, _):
            for k in range(2):
                self.ring_copy(k, i, i).wait_send()
                self.sib_copy(k, i).wait_send()
            return 0

        lax.fori_loop(0, CHIPS - 1, body, 0)
        for k in range(2):
            self.sib_copy(k, CHIPS - 1).wait_send()


def kernel(names, *refs):
    r = types.SimpleNamespace(**dict(zip(names, refs, strict=True)))
    p = Place()
    z, core = p.z, p.core
    scale = 1.0 / HEAD_DIM**0.5
    width = r.wkv.shape[2]
    heads = width // HEAD_DIM
    model = r.wout.shape[1]
    enc_width = r.wkv.shape[1]
    half_model = model // 2
    half_rows = NLEN // 2
    x, y = p.seq // 4, lax.rem(p.seq, 4)

    loads = []
    for j, (src, dst) in enumerate(
        (
            (r.nbr_in, r.nbr_raw),
            (r.wq_in, r.wq_all.at[z]),
            (r.wo_in, r.wo_all.at[z]),
            (r.tok_in.at[:, pl.ds(0, half_model)], r.tok_all.at[0, p.me]),
            (r.tok_in.at[:, pl.ds(half_model, half_model)], r.tok_all.at[1, p.me]),
            (r.dec_in, r.wdec),
            (r.wkv_in, r.wkv_raw),
            (r.wout_in, r.wout),
        )
    ):
        c = pltpu.make_async_copy(src, dst, r.load_sems.at[j])
        c.start()
        loads.append(c)
    load_nbr, load_q, load_o, load_tok0, load_tok1, load_dec, load_kv, load_out = loads

    def to_x(shift):
        return {"seq": 4 * lax.rem(x + shift + 4, 4) + y}

    def to_y(shift):
        return {"seq": 4 * x + lax.rem(y + shift + 4, 4)}

    ahead = lax.rem(p.seq + 1, p.n_seq)
    behind = lax.rem(p.seq + p.n_seq - 1, p.n_seq)
    partners = [p.on(z + h) for h in range(1, CHIPS)]
    partners += [{"nbr": p.sibling}, to_x(1), to_x(-1), to_y(1), to_y(-1), {"seq": ahead}, {"seq": behind}]
    barrier = pltpu.get_barrier_semaphore()
    for who in partners:
        pl.semaphore_signal(barrier, inc=1, device_id=who, device_id_type=MESH)
    load_nbr.wait()
    r.nbr32[...] = r.nbr_raw[...].astype(F32)
    for c in range(CHIPS):
        pair = [r.nbr32[lax.rem(r.table[k, c], r.nbr32.shape[0])] for k in range(2)]
        r.nbr_send[c] = jnp.concatenate(pair, axis=0).astype(BF16)
    r.nbr_all[z, core] = r.nbr_send[z]
    for c in (load_q, load_o, load_tok0, load_tok1):
        c.wait()
    pl.semaphore_wait(barrier, len(partners))

    def query_piece(chip, a):
        rows = pl.ds(pl.multiple_of(224 * y + 112 * (a // 2), 16), 112)
        return r.wq_all.at[chip, rows, pl.ds(pl.multiple_of(128 * lax.rem(a, 2), 128), 128)]

    def query_slab(chip, b):
        return r.wq_all.at[chip, pl.ds(pl.multiple_of(224 * b, 16), 224)]

    def out_piece(chip, a):
        return r.wo_all.at[chip, pl.ds(pl.multiple_of(64 * x + 16 * a, 16), 16)]

    def out_slab(chip, b):
        return r.wo_all.at[chip, pl.ds(pl.multiple_of(64 * b, 16), 64)]

    def stream(name, k, ref, sibling=True):
        sems = [getattr(r, name + end).at[k] for end in ("_f", "_r", "_s")[: 2 + sibling]]
        return Gather(p, ref, *sems)

    tok, enc = ([stream(name, k, getattr(r, name + "_all").at[k].at.__getitem__) for k in range(2)] for name in ("tok", "enc"))
    weights_z = [
        stream("wz", 0, lambda slot: query_piece(slot // 2, x), False),
        stream("wz", 1, lambda slot: out_piece(slot // 2, y), False),
    ]
    spread_sems = [getattr(r, "x" + c) for c in "abcdefgh"]
    weights_xy = [
        Spread(p, query_piece, query_slab, (x, to_x), (y, to_y), [s.at[0] for s in spread_sems]),
        Spread(p, out_piece, out_slab, (y, to_y), (x, to_x), [s.at[1] for s in spread_sems]),
    ]

    def weights(what, *items):
        for i in items:
            for w in weights_xy:
                getattr(w, what)(i)

    def weights_step(h):
        for w in weights_z:
            w.step(h)

    def remote(src, dst, target, send, recv):
        return pltpu.make_async_remote_copy(
            src_ref=src, dst_ref=dst, send_sem=send, recv_sem=recv, device_id=target, device_id_type=MESH
        )

    def halo(src, dst, target, j):
        return remote(src, dst, {"seq": target}, r.halo_sems.at[2 * j], r.halo_sems.at[2 * j + 1])

    send_q = halo(r.hq, r.hq_got, behind, 0)
    send_a = halo(r.ha, r.ha_got, ahead, 1)

    def nbr_copy(h):
        return remote(
            r.nbr_send.at[wrap(z + h)], r.nbr_all.at[z, core], p.on(z + h), r.nbr_sems.at[0, h], r.nbr_sems.at[1, z]
        )

    def nbr_arrived(h):
        chip = wrap(z + h)
        remote(
            r.nbr_send.at[0], r.nbr_all.at[chip, core], p.on(chip), r.nbr_sems.at[0, 0], r.nbr_sems.at[1, chip]
        ).wait_recv()

    nbr_sib = remote(
        r.nbr_all.at[:, core], r.nbr_all.at[:, core], {"nbr": p.sibling}, r.pair_sems.at[0], r.pair_sems.at[1]
    )
    nbr_sib_in = remote(
        r.nbr_all.at[:, 1 - core], r.nbr_all.at[:, 1 - core], {"nbr": p.sibling}, r.pair_sems.at[0], r.pair_sems.at[1]
    )

    def cond_copy(j, h):
        return remote(
            r.cond.at[j, wrap(z + h)], r.cond_got.at[z, j], p.on(z + h), r.cond_s.at[j, h], r.cond_r.at[j, z]
        )

    def cond_arrived(j, chip):
        remote(
            r.cond.at[j, 0], r.cond_got.at[chip, j], p.on(chip), r.cond_s.at[j, 0], r.cond_r.at[j, chip]
        ).wait_recv()

    order = (1, -1, 2, -2, 3, -3, 4)

    def project(j):
        x0, x1 = (r.tok_all[k].reshape(CHIPS * GROUP, half_model) for k in range(2))
        return dot(x0, r.wdec[j, pl.ds(0, half_model)]) + dot(x1, r.wdec[j, pl.ds(half_model, half_model)])

    def make_cond(*shifts):
        chips = [wrap(z + h) for h in shifts]
        for t in tok:
            for c in chips:
                t.from_sibling(c)
        x = [
            jnp.concatenate([r.tok_all[k, pl.ds(2 * c, 2)].reshape(GROUP, half_model) for c in chips], axis=0)
            for k in range(2)
        ]
        for j in range(2):
            y = sum(dot(x[k], r.wdec[1 + j, pl.ds(k * half_model, half_model)]) for k in range(2)).astype(BF16)
            for n, (h, c) in enumerate(zip(shifts, chips, strict=True)):
                part = y[GROUP * n : GROUP * (n + 1)]
                if h == 0:
                    r.cond_got[z, j] = part
                else:
                    r.cond[j, c] = part
                    cond_copy(j, h % CHIPS).start()

    def encode(*items):
        chips = [p.nth(i) for i in items]
        for i, chip in zip(items, chips, strict=True):
            if i > 0:
                for j in range(2):
                    cond_arrived(j, chip)
                for w in weights_xy:
                    w.ready(i)
        rows = r.nbr_all[...].reshape(2 * NLEN, enc_width)
        term = 0.0
        for chip in chips:
            queries = dot(rows, r.wq_all[chip]).astype(BF16)
            per_head = []
            for h in range(heads):
                cols = slice(HEAD_DIM * h, HEAD_DIM * (h + 1))
                shares = softmax(dot_t(queries[:, cols], r.cond_got[chip, 0, :, cols]) * scale)
                per_head.append(dot(shares, r.cond_got[chip, 1, :, cols]).astype(BF16))
            term += dot(jnp.concatenate(per_head, axis=1), r.wo_all[chip])
        if 0 in items:
            r.enc_sum[...] = term
        else:
            r.enc_sum[...] += term

    def of_slot(rows, slot):
        rows = rows.reshape(16, 2, 8, enc_width)
        return jnp.where(slot == 0, rows[:, 0], rows[:, 1]).reshape(NLEN, enc_width)

    sum_copy = remote(r.sum_out, r.sum_got, {"nbr": p.sibling}, r.pair_sems.at[2], r.pair_sems.at[3])

    def split_kv():
        step = 128

        def body(i, _):
            mine = pl.ds(pl.multiple_of(i * step, step), step)
            both = r.wkv_raw[mine].astype(F32)
            r.wkv[0, mine] = both[:, 0].astype(BF16)
            r.wkv[1, mine] = both[:, 1].astype(BF16)
            return 0

        lax.fori_loop(0, enc_width // step, body, 0)

    def make_kv(k, g):
        rows = r.enc_all[k, pl.ds(2 * g, 2)].reshape(NLEN, enc_width)
        for j in range(2):
            r.kv[j, g, pl.ds(NLEN * k, NLEN)] = dot(rows, r.wkv[j]).astype(BF16)

    def attend(g):
        queries = r.qpad[pl.ds(pl.multiple_of(GROUP * (g + 1), GROUP), GROUP), :]
        own = (lax.broadcasted_iota(jnp.int32, queries.shape, 0) == 0) | (g != CHIPS - 1)
        queries = jnp.where(own, queries, r.hq_got[...].astype(F32)).astype(BF16)
        count = r.counts[p.seq * CHIPS + g]
        key = lax.broadcasted_iota(jnp.int32, (GROUP, 2 * NLEN), 1)
        live = lax.rem(key // half_rows, 2) < count
        per_head = []
        for h in range(heads):
            cols = slice(HEAD_DIM * h, HEAD_DIM * (h + 1))
            scores = jnp.where(live, dot_t(queries[:, cols], r.kv[0, g, :, cols]) * scale, -1e30)
            per_head.append(dot(softmax(scores), r.kv[1, g, :, cols]))
        got = jnp.concatenate(per_head, axis=1).astype(BF16)
        r.att[pl.ds(pl.multiple_of(GROUP * (g + 1), GROUP), GROUP), :] = got.astype(F32)

        @pl.when(g == CHIPS - 1)
        def _():
            r.ha[...] = got
            send_a.start()

    def attend_all(first, count):
        def body(i, _):
            make_kv(1, p.nth(i))
            attend(p.nth(i))
            return 0

        lax.fori_loop(first, first + count, body, 0)

    out_sum = Reduce(p, r.opart, r.osib, r.obox, r.oout, (r.o0, r.o1, r.o2, r.o3))
    half = GROUP // 2
    block = 512

    def make_out(c):
        @pl.when(c == 0)
        def _():
            send_a.wait_recv()
            begins = lax.rem(p.seq * (GROUP * CHIPS), SEQ_LEN) == 0
            r.att[pl.ds(0, GROUP), :] = jnp.where(begins, 0.0, r.ha_got[...].astype(F32))

        wide = r.att[pl.ds(pl.multiple_of(GROUP * c, GROUP), GROUP + 8), :]
        rows = wide[1 : GROUP + 1].astype(BF16)

        for k in range(2):

            def body(j, _, k=k):
                cols = pl.ds(pl.multiple_of(j * block, block), block)
                weight = r.wout[:, pl.ds(pl.multiple_of(k * half_model + j * block, block), block)]
                y = dot(rows, weight).astype(BF16)
                r.opart[k, c, 0, :, cols] = y[:half]
                r.opart[k, c, 1, :, cols] = y[half:]
                return 0

            lax.fori_loop(0, half_model // block, body, 0)
            out_sum.sib_copy(k, c).start()

    def make_outs(chips):
        for c in chips:
            make_out(wrap(c))

    for g in (*weights_z, *tok):
        g.own()
    weights_step(1)
    weights("pieces_out", 1, 2)
    load_kv.wait()
    split_kv()
    weights_step(2)
    weights("pieces_out", 3, 4)
    weights("pieces_on", 1, 2)
    tok[0].step(1)
    tok[1].step(1)
    weights_step(3)
    weights("pieces_out", 5, 6)
    weights("slabs_out", 1, 2)
    weights("pieces_on", 3, 4)
    weights_step(4)
    weights("pieces_out", 7)
    weights("slabs_out", 3)
    weights("pieces_on", 5, 6)
    for h in order:
        nbr_copy(h % CHIPS).start()
    load_dec.wait()
    make_cond(0)
    tok[0].step(2)
    tok[1].step(2)
    weights("slabs_on", 1)
    weights("slabs_out", 4)
    weights("pieces_on", 7)
    weights("slabs_on", 2)
    weights("slabs_out", 5)
    make_cond(1, -1)
    tok[0].step(3)
    tok[1].step(3)
    weights("slabs_on", 3)
    weights("slabs_out", 6)
    make_cond(2, -2)
    weights("slabs_on", 4)
    weights("slabs_out", 7)
    for h in order:
        nbr_arrived(h)
    nbr_sib.start()
    tok[0].step(4)
    tok[1].step(4)
    make_cond(3, -3)
    make_cond(4)
    weights("slabs_on", 5)
    nbr_sib_in.wait_recv()
    encode(0, 1, 2)
    weights("slabs_on", 6)
    encode(3, 4)
    weights("slabs_on", 7)
    encode(5, 6)
    encode(7)

    r.sum_out[...] = of_slot(r.enc_sum[...], 1 - core).astype(BF16)
    sum_copy.start()
    raw = of_slot(r.nbr_all[...].astype(F32).reshape(2 * NLEN, enc_width), core)
    mine = raw + of_slot(r.enc_sum[...], core)
    sum_copy.wait_recv()
    combined = mine + r.sum_got[...].astype(F32)
    factor = lax.rsqrt(jnp.mean(combined * combined, axis=-1, keepdims=True) + 1e-06)
    encoded = (combined * factor * r.gain[...].reshape(1, enc_width)).astype(BF16)
    for k in range(2):
        r.enc_all[k, p.me] = encoded[half_rows * k : half_rows * (k + 1)]
        enc[k].own()
    r.enc_ref[...] = encoded
    r.qpad[pl.ds(1, CHIPS * GROUP), :] = project(0).astype(BF16).astype(F32)
    r.hq[...] = r.qpad[pl.ds(0, GROUP), :].astype(BF16)
    send_q.start()
    load_out.wait()
    for h in (1, 2):
        for k in range(2):
            enc[k].step(h)
    send_q.wait_recv()
    for h in (0, 1, -1, 2, -2):
        enc[0].from_sibling(z + h)

    def first_kv(i, _):
        make_kv(0, p.nth(i))
        return 0

    lax.fori_loop(0, 5, first_kv, 0)
    for h in (0, 1, -1):
        enc[1].from_sibling(z + h)
    attend_all(0, 3)
    enc[0].step(3)
    enc[1].step(3)
    make_outs((z, z + 1))
    for h in (2, -2):
        enc[1].from_sibling(z + h)
    attend_all(3, 2)
    enc[0].step(4)
    enc[1].step(4)
    make_outs((z - 1, z + 2))
    for h in (3, -3, 4):
        enc[0].from_sibling(z + h)
    lax.fori_loop(5, CHIPS, first_kv, 0)
    for h in (3, -3):
        enc[1].from_sibling(z + h)
    attend_all(5, 2)
    enc[1].from_sibling(z + 4)
    attend_all(7, 1)
    make_outs((z + 4,))
    for k in range(2):
        out_sum.item(k, jnp.int32(0))
    make_outs((z - 3, z + 3, z - 2))

    def out_items(i, _):
        for k in range(2):
            out_sum.item(k, i)
        return 0

    lax.fori_loop(1, CHIPS - 1, out_items, 0)
    for k in range(2):
        r.out_ref[:, pl.ds(k * half_model, half_model)] = out_sum.total(k).astype(BF16)

    for g in (*tok, *enc, *weights_z, *weights_xy):
        g.drain()
    out_sum.drain()
    for h in range(1, CHIPS):
        nbr_copy(h).wait_send()
        for j in range(2):
            cond_copy(j, h).wait_send()
    for c in (nbr_sib, sum_copy, send_q, send_a):
        c.wait_send()


def local(
    tokens, nbr_embed, neighbour_table, valid_counts, dec_proj, enc_query, enc_out, enc_gain, nbr_proj, out_proj
):
    rows, model = tokens.shape
    nbrs, piece, enc_width = nbr_embed.shape
    width = enc_query.shape[1]
    block = 2 * piece
    sub = NLEN // 2
    padded = GROUP * (CHIPS + 1) + 8
    dma = pltpu.SemaphoreType.DMA
    half = (rows, model // 2)
    scratch = {
        "tok_all": pltpu.VMEM((2, 16, *half), BF16),
        "enc_all": pltpu.VMEM((2, 16, sub, enc_width), BF16),
        "nbr_all": pltpu.VMEM((CHIPS, 2, block, enc_width), BF16),
        "nbr_send": pltpu.VMEM((CHIPS, block, enc_width), BF16),
        "nbr_raw": pltpu.VMEM((nbrs, piece, enc_width), BF16),
        "nbr32": pltpu.VMEM((nbrs, piece, enc_width), F32),
        "wdec": pltpu.VMEM((3, model, width), BF16),
        "wq_all": pltpu.VMEM((CHIPS, enc_width, width), BF16),
        "wo_all": pltpu.VMEM((CHIPS, width, enc_width), BF16),
        "wkv_raw": pltpu.VMEM((enc_width, 2, width), BF16),
        "wkv": pltpu.VMEM((2, enc_width, width), BF16),
        "wout": pltpu.VMEM((width, model), BF16),
        "qpad": pltpu.VMEM((padded, width), F32),
        "cond": pltpu.VMEM((2, CHIPS, GROUP, width), BF16),
        "cond_got": pltpu.VMEM((CHIPS, 2, GROUP, width), BF16),
        "enc_sum": pltpu.VMEM((2 * NLEN, enc_width), F32),
        "sum_out": pltpu.VMEM((NLEN, enc_width), BF16),
        "sum_got": pltpu.VMEM((NLEN, enc_width), BF16),
        "kv": pltpu.VMEM((2, CHIPS, 2 * NLEN, width), BF16),
        "att": pltpu.VMEM((padded, width), F32),
        "opart": pltpu.VMEM((2, CHIPS, 2, *half), BF16),
        "osib": pltpu.VMEM((2, CHIPS, *half), BF16),
        "obox": pltpu.VMEM((2, CHIPS + 1, *half), BF16),
        "oout": pltpu.VMEM((2, CHIPS - 1, *half), BF16),
        **{name: pltpu.VMEM((GROUP, width), BF16) for name in ("hq", "hq_got", "ha", "ha_got")},
        "load_sems": dma((8,)),
        "halo_sems": dma((4,)),
        "nbr_sems": dma((2, CHIPS)),
        "pair_sems": dma((4,)),
        "cond_s": dma((2, CHIPS)),
        "cond_r": dma((2, CHIPS)),
        **{f"{name}_{x}": dma((2, n)) for name in ("tok", "enc", "wz") for x, n in (("f", 7), ("s", 8), ("r", 16))},
        **{f"x{c}": dma((2, CHIPS, 2)) if c in "abef" else dma((2, CHIPS)) for c in "abcdefgh"},
        **{f"o{j}": dma((2, n)) for j, n in enumerate((8, 8, 7, 9))},
    }
    inputs = {
        "tok_in": (tokens, pl.ANY),
        "nbr_in": (nbr_embed, pl.ANY),
        "table": (neighbour_table.T, pltpu.SMEM),
        "counts": (valid_counts, pltpu.SMEM),
        "dec_in": (jnp.transpose(dec_proj, (1, 0, 2)), pl.ANY),
        "wq_in": (enc_query, pl.ANY),
        "wo_in": (enc_out, pl.ANY),
        "gain": (enc_gain, pltpu.VMEM),
        "wkv_in": (nbr_proj, pl.ANY),
        "wout_in": (out_proj, pl.ANY),
    }
    vmem = pl.BlockSpec(memory_space=pltpu.VMEM)
    names = (*inputs, "out_ref", "enc_ref", *scratch)
    return pl.pallas_call(
        functools.partial(kernel, names),
        out_shape=(
            jax.ShapeDtypeStruct((rows, model), BF16),
            jax.ShapeDtypeStruct((NLEN, enc_width), BF16),
        ),
        in_specs=[pl.BlockSpec(memory_space=space) for _, space in inputs.values()],
        out_specs=(vmem, vmem),
        scratch_shapes=list(scratch.values()),
        compiler_params=pltpu.CompilerParams(
            collective_id=0, has_side_effects=True, vmem_limit_bytes=60 * 2**20
        ),
        name="retrieval",
    )(*(array for array, _ in inputs.values()))


def solution(mesh):
    return jax.shard_map(
        local,
        mesh=mesh,
        in_specs=(
            P(("seq", "nbr"), None),
            P("seq", "nbr", None),
            P("seq", None),
            P(),
            P(None, None, "nbr"),
            P(None, "nbr"),
            P("nbr", None),
            P(),
            P(None, None, "nbr"),
            P("nbr", None),
        ),
        out_specs=(P(("seq", "nbr"), None), P(("seq", "nbr"), None)),
        check_vma=False,
    )
```

```python
import functools
import types

import jax
import jax.numpy as jnp
from jax import lax
from jax.experimental import pallas as pl
from jax.experimental.pallas import tpu as pltpu
from jax.sharding import PartitionSpec as P

HEAD_DIM = 128
GROUP = 64
NLEN = 128
SEQ_LEN = 2048
CHIPS = 8
F32 = jnp.float32
BF16 = jnp.bfloat16
MESH = pl.DeviceIdType.MESH


def dot(a, b):
    return jnp.dot(a, b, preferred_element_type=F32)


def dot_t(a, b):
    return lax.dot_general(a, b, (((1,), (1,)), ((), ())), preferred_element_type=F32)


def softmax(scores):
    peak = jnp.max(scores, axis=-1, keepdims=True)
    raised = jnp.exp(scores - peak)
    return (raised * (1.0 / jnp.sum(raised, axis=-1, keepdims=True))).astype(BF16)


def wrap(x):
    return lax.rem(x + 2 * CHIPS, CHIPS)


class Place:
    def __init__(self):
        self.seq = lax.axis_index("seq")
        self.n_seq = lax.axis_size("seq")
        me = lax.axis_index("nbr")
        self.me = me
        self.z = me // 2
        self.core = lax.rem(me, 2)
        self.d = 1 - 2 * self.core
        self.sibling = me + self.d

    def on(self, chip):
        return {"nbr": 2 * wrap(chip) + self.core}

    def nth(self, i):
        sign = jnp.where(lax.rem(i, 2) == 1, 1, -1)
        return wrap(self.z + sign * ((i + 1) // 2))


class Gather:
    def __init__(self, place, ref, forward_sems, recv_sems, sibling_sems=None):
        self.p, self.ref = place, ref
        self.fs, self.rs, self.ss = forward_sems, recv_sems, sibling_sems
        self.sent = []

    def copy(self, chip, core, target, sem):
        slot = 2 * wrap(chip) + core
        return pltpu.make_async_remote_copy(
            src_ref=self.ref(slot),
            dst_ref=self.ref(slot),
            send_sem=sem,
            recv_sem=self.rs.at[slot],
            device_id=target,
            device_id_type=MESH,
        )

    def start(self, chip, target, sem):
        c = self.copy(chip, self.p.core, target, sem)
        c.start()
        self.sent.append(c)

    def to_sibling(self, chip, i):
        if self.ss is not None:
            self.start(chip, {"nbr": self.p.sibling}, self.ss.at[i])

    def arrived(self, chip):
        self.copy(chip, self.p.core, {"nbr": self.p.sibling}, self.fs.at[0]).wait_recv()

    def from_sibling(self, chip):
        self.copy(chip, 1 - self.p.core, {"nbr": self.p.sibling}, self.fs.at[0]).wait_recv()

    def own(self):
        z = self.p.z
        self.start(z, self.p.on(z + 1), self.fs.at[0])
        self.start(z, self.p.on(z - 1), self.fs.at[1])
        self.to_sibling(z, 0)

    def step(self, h):
        z, d = self.p.z, self.p.d
        if h < 3:
            for j, sign in enumerate((1, -1)):
                self.arrived(z - sign * h)
                self.start(z - sign * h, self.p.on(z + sign), self.fs.at[2 * h + j])
                self.to_sibling(z - sign * h, 2 * h - 1 + j)
        elif h == 3:
            self.arrived(z - 3 * d)
            self.start(z - 3 * d, self.p.on(z + d), self.fs.at[6])
            self.to_sibling(z - 3 * d, 5)
            self.arrived(z + 3 * d)
            self.to_sibling(z + 3 * d, 6)
        else:
            self.arrived(z + 4)
            self.to_sibling(z + 4, 7)

    def drain(self):
        for c in self.sent:
            c.wait_send()


class Spread:
    def __init__(self, place, piece, slab, first, second, sems):
        self.p, self.piece, self.slab = place, piece, slab
        (self.a, self.to_first), (self.b, self.to_second) = first, second
        self.bs, self.br, self.cs, self.cr, self.ds, self.dr, self.es, self.er = sems
        self.sent = []

    def copy(self, ref, target, send, recv):
        return pltpu.make_async_remote_copy(
            src_ref=ref, dst_ref=ref, send_sem=send, recv_sem=recv, device_id=target, device_id_type=MESH
        )

    def start(self, *copy):
        c = self.copy(*copy)
        c.start()
        self.sent.append(c)

    def send_both(self, i, ref, to, send, recv):
        for j, sign in enumerate((1, -1)):
            self.start(ref, to(sign), send.at[i, j], recv.at[i, j])

    def pass_on(self, i, ref, to, arrived, send, recv):
        for j, sign in enumerate((1, -1)):
            self.copy(ref(-sign), to(sign), send.at[i], arrived.at[i, j]).wait_recv()
        sign = 1 if i % 2 else -1
        self.start(ref(-sign), to(sign), send.at[i], recv.at[i])

    def piece_at(self, i, shift):
        return self.piece(self.p.nth(i), lax.rem(self.a + shift + 4, 4))

    def slab_at(self, i, shift):
        return self.slab(self.p.nth(i), lax.rem(self.b + shift + 4, 4))

    def pieces_out(self, i):
        self.send_both(i, self.piece_at(i, 0), self.to_first, self.bs, self.br)

    def pieces_on(self, i):
        self.pass_on(i, functools.partial(self.piece_at, i), self.to_first, self.br, self.cs, self.cr)

    def slabs_out(self, i):
        self.copy(self.piece_at(i, 2), self.to_first(1), self.cs.at[i], self.cr.at[i]).wait_recv()
        self.send_both(i, self.slab_at(i, 0), self.to_second, self.ds, self.dr)

    def slabs_on(self, i):
        self.pass_on(i, functools.partial(self.slab_at, i), self.to_second, self.dr, self.es, self.er)

    def ready(self, i):
        self.copy(self.slab_at(i, 2), self.to_second(1), self.es.at[i], self.er.at[i]).wait_recv()

    def drain(self):
        for c in self.sent:
            c.wait_send()


class Reduce:
    def __init__(self, place, part, from_sib, box, out, sems):
        self.p, self.part, self.from_sib, self.box, self.out = place, part, from_sib, box, out
        self.sib_send, self.sib_recv, self.send, self.recv = sems

    def sign(self, i):
        return jnp.where((i == 0) | (lax.rem(i, 2) == 1), self.p.d, -self.p.d)

    def dest(self, i):
        return wrap(self.p.z + self.sign(i) * (4 - (i + 1) // 2))

    def sib_copy(self, k, c):
        return pltpu.make_async_remote_copy(
            src_ref=self.part.at[k, c, 1 - self.p.core],
            dst_ref=self.from_sib.at[k, c],
            send_sem=self.sib_send.at[k, c],
            recv_sem=self.sib_recv.at[k, c],
            device_id={"nbr": self.p.sibling},
            device_id_type=MESH,
        )

    def ring_copy(self, k, i, land):
        return pltpu.make_async_remote_copy(
            src_ref=self.out.at[k, i],
            dst_ref=self.box.at[k, land],
            send_sem=self.send.at[k, i],
            recv_sem=self.recv.at[k, land],
            device_id=self.p.on(self.p.z + self.sign(i)),
            device_id_type=MESH,
        )

    def chip_sum(self, k, i):
        c = self.dest(i)
        return self.part[k, c, self.p.core].astype(F32) + self.from_sib[k, c].astype(F32)

    def item(self, k, i):
        self.sib_copy(k, self.dest(i)).wait_recv()
        starts = (i == 0) | (i == 2)

        @pl.when(starts)
        def _():
            self.out[k, i] = self.chip_sum(k, i).astype(BF16)

        @pl.when(jnp.logical_not(starts))
        def _():
            self.ring_copy(k, i, i).wait_recv()
            self.out[k, i] = (self.chip_sum(k, i) + self.box[k, i].astype(F32)).astype(BF16)

        self.ring_copy(k, i, jnp.where(i == 0, 1, i + 2)).start()

    def total(self, k):
        self.sib_copy(k, self.p.z).wait_recv()
        self.ring_copy(k, 0, 7).wait_recv()
        self.ring_copy(k, 0, 8).wait_recv()
        return self.chip_sum(k, jnp.int32(7)) + self.box[k, 7].astype(F32) + self.box[k, 8].astype(F32)

    def drain(self):
        def body(i, _):
            for k in range(2):
                self.ring_copy(k, i, i).wait_send()
                self.sib_copy(k, i).wait_send()
            return 0

        lax.fori_loop(0, CHIPS - 1, body, 0)
        for k in range(2):
            self.sib_copy(k, CHIPS - 1).wait_send()


def kernel(names, *refs):
    r = types.SimpleNamespace(**dict(zip(names, refs, strict=True)))
    p = Place()
    z, core = p.z, p.core
    scale = 1.0 / HEAD_DIM**0.5
    width = r.wkv.shape[2]
    heads = width // HEAD_DIM
    model = r.wout.shape[1]
    enc_width = r.wkv.shape[1]
    half_model = model // 2
    half_rows = NLEN // 2
    x, y = p.seq // 4, lax.rem(p.seq, 4)

    loads = []
    for j, (src, dst) in enumerate(
        (
            (r.nbr_in, r.nbr_raw),
            (r.wq_in, r.wq_all.at[z]),
            (r.wo_in, r.wo_all.at[z]),
            (r.tok_in.at[:, pl.ds(0, half_model)], r.tok_all.at[0, p.me]),
            (r.tok_in.at[:, pl.ds(half_model, half_model)], r.tok_all.at[1, p.me]),
            (r.dec_in, r.wdec),
            (r.wkv_in, r.wkv_raw),
            (r.wout_in, r.wout),
        )
    ):
        c = pltpu.make_async_copy(src, dst, r.load_sems.at[j])
        c.start()
        loads.append(c)
    load_nbr, load_q, load_o, load_tok0, load_tok1, load_dec, load_kv, load_out = loads

    def to_x(shift):
        return {"seq": 4 * lax.rem(x + shift + 4, 4) + y}

    def to_y(shift):
        return {"seq": 4 * x + lax.rem(y + shift + 4, 4)}

    ahead = lax.rem(p.seq + 1, p.n_seq)
    behind = lax.rem(p.seq + p.n_seq - 1, p.n_seq)
    partners = [p.on(z + h) for h in range(1, CHIPS)]
    partners += [{"nbr": p.sibling}, to_x(1), to_x(-1), to_y(1), to_y(-1), {"seq": ahead}, {"seq": behind}]
    barrier = pltpu.get_barrier_semaphore()
    for who in partners:
        pl.semaphore_signal(barrier, inc=1, device_id=who, device_id_type=MESH)
    load_nbr.wait()
    r.nbr32[...] = r.nbr_raw[...].astype(F32)
    for c in range(CHIPS):
        pair = [r.nbr32[lax.rem(r.table[k, c], r.nbr32.shape[0])] for k in range(2)]
        r.nbr_send[c] = jnp.concatenate(pair, axis=0).astype(BF16)
    r.nbr_all[z, core] = r.nbr_send[z]
    for c in (load_q, load_o, load_tok0, load_tok1):
        c.wait()
    pl.semaphore_wait(barrier, len(partners))

    def query_piece(chip, a):
        rows = pl.ds(pl.multiple_of(224 * y + 112 * (a // 2), 16), 112)
        return r.wq_all.at[chip, rows, pl.ds(pl.multiple_of(128 * lax.rem(a, 2), 128), 128)]

    def query_slab(chip, b):
        return r.wq_all.at[chip, pl.ds(pl.multiple_of(224 * b, 16), 224)]

    def out_piece(chip, a):
        return r.wo_all.at[chip, pl.ds(pl.multiple_of(64 * x + 16 * a, 16), 16)]

    def out_slab(chip, b):
        return r.wo_all.at[chip, pl.ds(pl.multiple_of(64 * b, 16), 64)]

    def stream(name, k, ref, sibling=True):
        sems = [getattr(r, name + end).at[k] for end in ("_f", "_r", "_s")[: 2 + sibling]]
        return Gather(p, ref, *sems)

    tok, enc = ([stream(name, k, getattr(r, name + "_all").at[k].at.__getitem__) for k in range(2)] for name in ("tok", "enc"))
    weights_z = [
        stream("wz", 0, lambda slot: query_piece(slot // 2, x), False),
        stream("wz", 1, lambda slot: out_piece(slot // 2, y), False),
    ]
    spread_sems = [getattr(r, "x" + c) for c in "abcdefgh"]
    weights_xy = [
        Spread(p, query_piece, query_slab, (x, to_x), (y, to_y), [s.at[0] for s in spread_sems]),
        Spread(p, out_piece, out_slab, (y, to_y), (x, to_x), [s.at[1] for s in spread_sems]),
    ]

    def weights(what, *items):
        for i in items:
            for w in weights_xy:
                getattr(w, what)(i)

    def weights_step(h):
        for w in weights_z:
            w.step(h)

    def remote(src, dst, target, send, recv):
        return pltpu.make_async_remote_copy(
            src_ref=src, dst_ref=dst, send_sem=send, recv_sem=recv, device_id=target, device_id_type=MESH
        )

    def halo(src, dst, target, j):
        return remote(src, dst, {"seq": target}, r.halo_sems.at[2 * j], r.halo_sems.at[2 * j + 1])

    send_q = halo(r.hq, r.hq_got, behind, 0)
    send_a = halo(r.ha, r.ha_got, ahead, 1)

    def nbr_copy(h):
        return remote(
            r.nbr_send.at[wrap(z + h)], r.nbr_all.at[z, core], p.on(z + h), r.nbr_sems.at[0, h], r.nbr_sems.at[1, z]
        )

    def nbr_arrived(h):
        chip = wrap(z + h)
        remote(
            r.nbr_send.at[0], r.nbr_all.at[chip, core], p.on(chip), r.nbr_sems.at[0, 0], r.nbr_sems.at[1, chip]
        ).wait_recv()

    nbr_sib = remote(
        r.nbr_all.at[:, core], r.nbr_all.at[:, core], {"nbr": p.sibling}, r.pair_sems.at[0], r.pair_sems.at[1]
    )
    nbr_sib_in = remote(
        r.nbr_all.at[:, 1 - core], r.nbr_all.at[:, 1 - core], {"nbr": p.sibling}, r.pair_sems.at[0], r.pair_sems.at[1]
    )

    def cond_copy(j, h):
        return remote(
            r.cond.at[j, wrap(z + h)], r.cond_got.at[z, j], p.on(z + h), r.cond_s.at[j, h], r.cond_r.at[j, z]
        )

    def cond_arrived(j, chip):
        remote(
            r.cond.at[j, 0], r.cond_got.at[chip, j], p.on(chip), r.cond_s.at[j, 0], r.cond_r.at[j, chip]
        ).wait_recv()

    order = (1, -1, 2, -2, 3, -3, 4)

    def project(j):
        x0, x1 = (r.tok_all[k].reshape(CHIPS * GROUP, half_model) for k in range(2))
        return dot(x0, r.wdec[j, pl.ds(0, half_model)]) + dot(x1, r.wdec[j, pl.ds(half_model, half_model)])

    def make_cond(*shifts):
        chips = [wrap(z + h) for h in shifts]
        for t in tok:
            for c in chips:
                t.from_sibling(c)
        x = [
            jnp.concatenate([r.tok_all[k, pl.ds(2 * c, 2)].reshape(GROUP, half_model) for c in chips], axis=0)
            for k in range(2)
        ]
        for j in range(2):
            y = sum(dot(x[k], r.wdec[1 + j, pl.ds(k * half_model, half_model)]) for k in range(2)).astype(BF16)
            for n, (h, c) in enumerate(zip(shifts, chips, strict=True)):
                part = y[GROUP * n : GROUP * (n + 1)]
                if h == 0:
                    r.cond_got[z, j] = part
                else:
                    r.cond[j, c] = part
                    cond_copy(j, h % CHIPS).start()

    def encode(*items):
        chips = [p.nth(i) for i in items]
        for i, chip in zip(items, chips, strict=True):
            if i > 0:
                for j in range(2):
                    cond_arrived(j, chip)
                for w in weights_xy:
                    w.ready(i)
        rows = r.nbr_all[...].reshape(2 * NLEN, enc_width)
        term = 0.0
        for chip in chips:
            queries = dot(rows, r.wq_all[chip]).astype(BF16)
            per_head = []
            for h in range(heads):
                cols = slice(HEAD_DIM * h, HEAD_DIM * (h + 1))
                shares = softmax(dot_t(queries[:, cols], r.cond_got[chip, 0, :, cols]) * scale)
                per_head.append(dot(shares, r.cond_got[chip, 1, :, cols]).astype(BF16))
            term += dot(jnp.concatenate(per_head, axis=1), r.wo_all[chip])
        if 0 in items:
            r.enc_sum[...] = term
        else:
            r.enc_sum[...] += term

    def of_slot(rows, slot):
        rows = rows.reshape(16, 2, 8, enc_width)
        return jnp.where(slot == 0, rows[:, 0], rows[:, 1]).reshape(NLEN, enc_width)

    def sum_copy(k):
        sems = r.pair_sems.at[2 + 2 * k], r.pair_sems.at[3 + 2 * k]
        return remote(r.sum_out.at[k], r.sum_got.at[k], {"nbr": p.sibling}, *sems)


    def split_kv():
        step = 128

        def body(i, _):
            mine = pl.ds(pl.multiple_of(i * step, step), step)
            both = r.wkv_raw[mine].astype(F32)
            r.wkv[0, mine] = both[:, 0].astype(BF16)
            r.wkv[1, mine] = both[:, 1].astype(BF16)
            return 0

        lax.fori_loop(0, enc_width // step, body, 0)

    def attend(*shifts):
        groups = [wrap(z + h) for h in shifts]
        for h in shifts:
            for k in range(2):
                enc[k].from_sibling(z + h)
        key = lax.broadcasted_iota(jnp.int32, (GROUP, 2 * NLEN), 1)
        slot = lax.rem(key // half_rows, 2)
        got = []
        for g in groups:
            rows = r.enc_all[:, pl.ds(2 * g, 2)].reshape(2 * NLEN, enc_width)
            keys, values = (dot(rows, r.wkv[j]).astype(BF16) for j in range(2))
            queries = r.qpad[pl.ds(pl.multiple_of(GROUP * (g + 1), GROUP), GROUP), :]
            own = (lax.broadcasted_iota(jnp.int32, queries.shape, 0) == 0) | (g != CHIPS - 1)
            queries = jnp.where(own, queries, r.hq_got[...].astype(F32)).astype(BF16)
            live = slot < r.counts[p.seq * CHIPS + g]
            per_head = []
            for h in range(heads):
                cols = slice(HEAD_DIM * h, HEAD_DIM * (h + 1))
                scores = jnp.where(live, dot_t(queries[:, cols], keys[:, cols]) * scale, -1e30)
                per_head.append(dot(softmax(scores), values[:, cols]))
            got.append(jnp.concatenate(per_head, axis=1).astype(BF16))
        for g, rows in zip(groups, got, strict=True):
            r.att[pl.ds(pl.multiple_of(GROUP * (g + 1), GROUP), GROUP), :] = rows.astype(F32)
        for g in groups:

            @pl.when(g == CHIPS - 1)
            def _():
                r.ha[...] = r.att[pl.ds(GROUP * CHIPS, GROUP), :].astype(BF16)
                send_a.start()

    out_sum = Reduce(p, r.opart, r.osib, r.obox, r.oout, (r.o0, r.o1, r.o2, r.o3))
    half = GROUP // 2
    block = 512

    def make_out(c):
        @pl.when(c == 0)
        def _():
            send_a.wait_recv()
            begins = lax.rem(p.seq * (GROUP * CHIPS), SEQ_LEN) == 0
            r.att[pl.ds(0, GROUP), :] = jnp.where(begins, 0.0, r.ha_got[...].astype(F32))

        wide = r.att[pl.ds(pl.multiple_of(GROUP * c, GROUP), GROUP + 8), :]
        rows = wide[1 : GROUP + 1].astype(BF16)

        for k in range(2):

            def body(j, _, k=k):
                cols = pl.ds(pl.multiple_of(j * block, block), block)
                weight = r.wout[:, pl.ds(pl.multiple_of(k * half_model + j * block, block), block)]
                y = dot(rows, weight).astype(BF16)
                r.opart[k, c, 0, :, cols] = y[:half]
                r.opart[k, c, 1, :, cols] = y[half:]
                return 0

            lax.fori_loop(0, half_model // block, body, 0)
            out_sum.sib_copy(k, c).start()

    def make_outs(chips):
        for c in chips:
            make_out(wrap(c))

    for g in (*weights_z, *tok):
        g.own()
    weights_step(1)
    weights("pieces_out", 1, 2)
    load_kv.wait()
    split_kv()
    weights_step(2)
    weights("pieces_out", 3, 4)
    weights("pieces_on", 1, 2)
    tok[0].step(1)
    tok[1].step(1)
    weights_step(3)
    weights("pieces_out", 5, 6)
    weights("slabs_out", 1, 2)
    weights("pieces_on", 3, 4)
    weights_step(4)
    weights("pieces_out", 7)
    weights("slabs_out", 3)
    weights("pieces_on", 5, 6)
    for h in order:
        nbr_copy(h % CHIPS).start()
    load_dec.wait()
    make_cond(0)
    tok[0].step(2)
    tok[1].step(2)
    weights("slabs_on", 1)
    weights("slabs_out", 4)
    weights("pieces_on", 7)
    weights("slabs_on", 2)
    weights("slabs_out", 5)
    make_cond(1, -1)
    tok[0].step(3)
    tok[1].step(3)
    for h in order:
        nbr_arrived(h)
    nbr_sib.start()
    weights("slabs_on", 3)
    weights("slabs_out", 6)
    make_cond(2, -2)
    weights("slabs_on", 4)
    weights("slabs_out", 7)
    nbr_sib_in.wait_recv()
    encode(0, 1, 2)
    tok[0].step(4)
    tok[1].step(4)
    make_cond(3, -3)
    make_cond(4)
    weights("slabs_on", 5)
    weights("slabs_on", 6)
    encode(3, 4)
    weights("slabs_on", 7)
    encode(5, 6)
    encode(7)

    theirs = of_slot(r.enc_sum[...], 1 - core)
    for k in range(2):
        r.sum_out[k] = theirs[half_rows * k : half_rows * (k + 1)].astype(BF16)
        sum_copy(k).start()
    mine = of_slot(r.nbr_all[...].astype(F32).reshape(2 * NLEN, enc_width), core) + of_slot(r.enc_sum[...], core)
    gain = r.gain[...].reshape(1, enc_width)
    for k in range(2):
        sum_copy(k).wait_recv()
        rows = slice(half_rows * k, half_rows * (k + 1))
        combined = mine[rows] + r.sum_got[k].astype(F32)
        factor = lax.rsqrt(jnp.mean(combined * combined, axis=-1, keepdims=True) + 1e-06)
        encoded = (combined * factor * gain).astype(BF16)
        r.enc_all[k, p.me] = encoded
        enc[k].own()
        r.enc_ref[rows] = encoded
    r.qpad[pl.ds(1, CHIPS * GROUP), :] = project(0).astype(BF16).astype(F32)
    r.hq[...] = r.qpad[pl.ds(0, GROUP), :].astype(BF16)
    send_q.start()
    load_out.wait()
    def enc_step(h):
        for k in range(2):
            enc[k].step(h)

    enc_step(1)
    send_q.wait_recv()
    attend(0)
    enc_step(2)
    attend(1, -1)
    make_outs((z, z + 1))
    enc_step(3)
    attend(2, -2)
    attend(3, -3)
    enc_step(4)
    attend(4)
    make_outs((z + 4,))

    def out_items(*items):
        for i in items:
            for k in range(2):
                out_sum.item(k, jnp.int32(i))

    out_items(0)
    make_outs((z + 3, z - 3))
    out_items(2)
    out_items(1)
    make_outs((z + 2, z - 2))
    out_items(4)
    out_items(3)
    make_outs((z - 1,))
    out_items(6, 5)
    for k in range(2):
        r.out_ref[:, pl.ds(k * half_model, half_model)] = out_sum.total(k).astype(BF16)

    for g in (*tok, *enc, *weights_z, *weights_xy):
        g.drain()
    out_sum.drain()
    for h in range(1, CHIPS):
        nbr_copy(h).wait_send()
        for j in range(2):
            cond_copy(j, h).wait_send()
    for c in (nbr_sib, sum_copy(0), sum_copy(1), send_q, send_a):
        c.wait_send()


def hand_out(out_in, enc_in, out_ref, enc_ref, sems):
    copies = [
        pltpu.make_async_copy(out_in, out_ref, sems.at[0]),
        pltpu.make_async_copy(enc_in, enc_ref, sems.at[1]),
    ]
    for c in copies:
        c.start()
    for c in copies:
        c.wait()


def local(
    tokens, nbr_embed, neighbour_table, valid_counts, dec_proj, enc_query, enc_out, enc_gain, nbr_proj, out_proj
):
    rows, model = tokens.shape
    nbrs, piece, enc_width = nbr_embed.shape
    width = enc_query.shape[1]
    block = 2 * piece
    sub = NLEN // 2
    padded = GROUP * (CHIPS + 1) + 8
    dma = pltpu.SemaphoreType.DMA
    half = (rows, model // 2)
    scratch = {
        "tok_all": pltpu.VMEM((2, 16, *half), BF16),
        "enc_all": pltpu.VMEM((2, 16, sub, enc_width), BF16),
        "nbr_all": pltpu.VMEM((CHIPS, 2, block, enc_width), BF16),
        "nbr_send": pltpu.VMEM((CHIPS, block, enc_width), BF16),
        "nbr_raw": pltpu.VMEM((nbrs, piece, enc_width), BF16),
        "nbr32": pltpu.VMEM((nbrs, piece, enc_width), F32),
        "wdec": pltpu.VMEM((3, model, width), BF16),
        "wq_all": pltpu.VMEM((CHIPS, enc_width, width), BF16),
        "wo_all": pltpu.VMEM((CHIPS, width, enc_width), BF16),
        "wkv_raw": pltpu.VMEM((enc_width, 2, width), BF16),
        "wkv": pltpu.VMEM((2, enc_width, width), BF16),
        "wout": pltpu.VMEM((width, model), BF16),
        "qpad": pltpu.VMEM((padded, width), F32),
        "cond": pltpu.VMEM((2, CHIPS, GROUP, width), BF16),
        "cond_got": pltpu.VMEM((CHIPS, 2, GROUP, width), BF16),
        "enc_sum": pltpu.VMEM((2 * NLEN, enc_width), F32),
        "sum_out": pltpu.VMEM((2, sub, enc_width), BF16),
        "sum_got": pltpu.VMEM((2, sub, enc_width), BF16),
        "att": pltpu.VMEM((padded, width), F32),
        "opart": pltpu.VMEM((2, CHIPS, 2, *half), BF16),
        "osib": pltpu.VMEM((2, CHIPS, *half), BF16),
        "obox": pltpu.VMEM((2, CHIPS + 1, *half), BF16),
        "oout": pltpu.VMEM((2, CHIPS - 1, *half), BF16),
        **{name: pltpu.VMEM((GROUP, width), BF16) for name in ("hq", "hq_got", "ha", "ha_got")},
        "load_sems": dma((8,)),
        "halo_sems": dma((4,)),
        "nbr_sems": dma((2, CHIPS)),
        "pair_sems": dma((6,)),
        "cond_s": dma((2, CHIPS)),
        "cond_r": dma((2, CHIPS)),
        **{f"{name}_{x}": dma((2, n)) for name in ("tok", "enc", "wz") for x, n in (("f", 7), ("s", 8), ("r", 16))},
        **{f"x{c}": dma((2, CHIPS, 2)) if c in "abef" else dma((2, CHIPS)) for c in "abcdefgh"},
        **{f"o{j}": dma((2, n)) for j, n in enumerate((8, 8, 7, 9))},
    }
    inputs = {
        "tok_in": (tokens, pl.ANY),
        "nbr_in": (nbr_embed, pl.ANY),
        "table": (neighbour_table.T, pltpu.SMEM),
        "counts": (valid_counts, pltpu.SMEM),
        "dec_in": (jnp.transpose(dec_proj, (1, 0, 2)), pl.ANY),
        "wq_in": (enc_query, pl.ANY),
        "wo_in": (enc_out, pl.ANY),
        "gain": (enc_gain, pltpu.VMEM),
        "wkv_in": (nbr_proj, pl.ANY),
        "wout_in": (out_proj, pl.ANY),
    }
    vmem = pl.BlockSpec(memory_space=pltpu.VMEM)
    names = (*inputs, "out_ref", "enc_ref", *scratch)
    results = pl.pallas_call(
        functools.partial(kernel, names),
        out_shape=(
            jax.ShapeDtypeStruct((rows, model), BF16),
            jax.ShapeDtypeStruct((NLEN, enc_width), BF16),
        ),
        in_specs=[pl.BlockSpec(memory_space=space) for _, space in inputs.values()],
        out_specs=(vmem, vmem),
        scratch_shapes=list(scratch.values()),
        compiler_params=pltpu.CompilerParams(
            collective_id=0, has_side_effects=True, vmem_limit_bytes=60 * 2**20
        ),
        name="retrieval",
    )(*(array for array, _ in inputs.values()))
    any_space = pl.BlockSpec(memory_space=pl.ANY)
    return pl.pallas_call(
        hand_out,
        out_shape=tuple(jax.ShapeDtypeStruct(a.shape, a.dtype) for a in results),
        in_specs=[vmem] * 2,
        out_specs=(any_space,) * 2,
        scratch_shapes=[dma((2,))],
        name="hand_out",
    )(*results)


def solution(mesh):
    return jax.shard_map(
        local,
        mesh=mesh,
        in_specs=(
            P(("seq", "nbr"), None),
            P("seq", "nbr", None),
            P("seq", None),
            P(),
            P(None, None, "nbr"),
            P(None, "nbr"),
            P("nbr", None),
            P(),
            P(None, None, "nbr"),
            P("nbr", None),
        ),
        out_specs=(P(("seq", "nbr"), None), P(("seq", "nbr"), None)),
        check_vma=False,
    )
```

```python
import functools
import types

import jax
import jax.numpy as jnp
from jax import lax
from jax.experimental import pallas as pl
from jax.experimental.pallas import tpu as pltpu
from jax.sharding import PartitionSpec as P

HEAD_DIM = 128
GROUP = 64
NLEN = 128
SEQ_LEN = 2048
CHIPS = 8
F32 = jnp.float32
BF16 = jnp.bfloat16
MESH = pl.DeviceIdType.MESH


def dot(a, b):
    return jnp.dot(a, b, preferred_element_type=F32)


def dot_t(a, b):
    return lax.dot_general(a, b, (((1,), (1,)), ((), ())), preferred_element_type=F32)


def softmax(scores):
    peak = jnp.max(scores, axis=-1, keepdims=True)
    raised = jnp.exp(scores - peak)
    return (raised * (1.0 / jnp.sum(raised, axis=-1, keepdims=True))).astype(BF16)


def wrap(x):
    return lax.rem(x + 2 * CHIPS, CHIPS)


class Place:
    def __init__(self):
        self.seq = lax.axis_index("seq")
        self.n_seq = lax.axis_size("seq")
        me = lax.axis_index("nbr")
        self.me = me
        self.z = me // 2
        self.core = lax.rem(me, 2)
        self.d = 1 - 2 * self.core
        self.sibling = me + self.d

    def on(self, chip):
        return {"nbr": 2 * wrap(chip) + self.core}

    def nth(self, i):
        sign = jnp.where(lax.rem(i, 2) == 1, 1, -1)
        return wrap(self.z + sign * ((i + 1) // 2))


class Gather:
    def __init__(self, place, ref, forward_sems, recv_sems, sibling_sems=None):
        self.p, self.ref = place, ref
        self.fs, self.rs, self.ss = forward_sems, recv_sems, sibling_sems
        self.sent = []

    def copy(self, chip, core, target, sem):
        slot = 2 * wrap(chip) + core
        return pltpu.make_async_remote_copy(
            src_ref=self.ref(slot),
            dst_ref=self.ref(slot),
            send_sem=sem,
            recv_sem=self.rs.at[slot],
            device_id=target,
            device_id_type=MESH,
        )

    def start(self, chip, target, sem):
        c = self.copy(chip, self.p.core, target, sem)
        c.start()
        self.sent.append(c)

    def to_sibling(self, chip, i):
        if self.ss is not None:
            self.start(chip, {"nbr": self.p.sibling}, self.ss.at[i])

    def arrived(self, chip):
        self.copy(chip, self.p.core, {"nbr": self.p.sibling}, self.fs.at[0]).wait_recv()

    def from_sibling(self, chip):
        self.copy(chip, 1 - self.p.core, {"nbr": self.p.sibling}, self.fs.at[0]).wait_recv()

    def own(self):
        z = self.p.z
        self.start(z, self.p.on(z + 1), self.fs.at[0])
        self.start(z, self.p.on(z - 1), self.fs.at[1])
        self.to_sibling(z, 0)

    def step(self, h):
        z, d = self.p.z, self.p.d
        if h < 3:
            for j, sign in enumerate((1, -1)):
                self.arrived(z - sign * h)
                self.start(z - sign * h, self.p.on(z + sign), self.fs.at[2 * h + j])
                self.to_sibling(z - sign * h, 2 * h - 1 + j)
        elif h == 3:
            self.arrived(z - 3 * d)
            self.start(z - 3 * d, self.p.on(z + d), self.fs.at[6])
            self.to_sibling(z - 3 * d, 5)
            self.arrived(z + 3 * d)
            self.to_sibling(z + 3 * d, 6)
        else:
            self.arrived(z + 4)
            self.to_sibling(z + 4, 7)

    def drain(self):
        for c in self.sent:
            c.wait_send()


class Spread:
    def __init__(self, place, piece, slab, first, second, sems):
        self.p, self.piece, self.slab = place, piece, slab
        (self.a, self.to_first), (self.b, self.to_second) = first, second
        self.bs, self.br, self.cs, self.cr, self.ds, self.dr, self.es, self.er = sems
        self.sent = []

    def copy(self, ref, target, send, recv):
        return pltpu.make_async_remote_copy(
            src_ref=ref, dst_ref=ref, send_sem=send, recv_sem=recv, device_id=target, device_id_type=MESH
        )

    def start(self, *copy):
        c = self.copy(*copy)
        c.start()
        self.sent.append(c)

    def send_both(self, i, ref, to, send, recv):
        for j, sign in enumerate((1, -1)):
            self.start(ref, to(sign), send.at[i, j], recv.at[i, j])

    def pass_on(self, i, ref, to, arrived, send, recv):
        for j, sign in enumerate((1, -1)):
            self.copy(ref(-sign), to(sign), send.at[i], arrived.at[i, j]).wait_recv()
        sign = 1 if i % 2 else -1
        self.start(ref(-sign), to(sign), send.at[i], recv.at[i])

    def piece_at(self, i, shift):
        return self.piece(self.p.nth(i), lax.rem(self.a + shift + 4, 4))

    def slab_at(self, i, shift):
        return self.slab(self.p.nth(i), lax.rem(self.b + shift + 4, 4))

    def pieces_out(self, i):
        self.send_both(i, self.piece_at(i, 0), self.to_first, self.bs, self.br)

    def pieces_on(self, i):
        self.pass_on(i, functools.partial(self.piece_at, i), self.to_first, self.br, self.cs, self.cr)

    def slabs_out(self, i):
        self.copy(self.piece_at(i, 2), self.to_first(1), self.cs.at[i], self.cr.at[i]).wait_recv()
        self.send_both(i, self.slab_at(i, 0), self.to_second, self.ds, self.dr)

    def slabs_on(self, i):
        self.pass_on(i, functools.partial(self.slab_at, i), self.to_second, self.dr, self.es, self.er)

    def ready(self, i):
        self.copy(self.slab_at(i, 2), self.to_second(1), self.es.at[i], self.er.at[i]).wait_recv()

    def drain(self):
        for c in self.sent:
            c.wait_send()


class Reduce:
    def __init__(self, place, part, from_sib, box, out, sems):
        self.p, self.part, self.from_sib, self.box, self.out = place, part, from_sib, box, out
        self.sib_send, self.sib_recv, self.send, self.recv = sems

    def sign(self, i):
        return jnp.where((i == 0) | (lax.rem(i, 2) == 1), self.p.d, -self.p.d)

    def dest(self, i):
        return wrap(self.p.z + self.sign(i) * (4 - (i + 1) // 2))

    def sib_copy(self, k, c):
        return pltpu.make_async_remote_copy(
            src_ref=self.part.at[k, c, 1 - self.p.core],
            dst_ref=self.from_sib.at[k, c],
            send_sem=self.sib_send.at[k, c],
            recv_sem=self.sib_recv.at[k, c],
            device_id={"nbr": self.p.sibling},
            device_id_type=MESH,
        )

    def ring_copy(self, k, i, land):
        return pltpu.make_async_remote_copy(
            src_ref=self.out.at[k, i],
            dst_ref=self.box.at[k, land],
            send_sem=self.send.at[k, i],
            recv_sem=self.recv.at[k, land],
            device_id=self.p.on(self.p.z + self.sign(i)),
            device_id_type=MESH,
        )

    def chip_sum(self, k, i):
        c = self.dest(i)
        return self.part[k, c, self.p.core].astype(F32) + self.from_sib[k, c].astype(F32)

    def item(self, k, i):
        self.sib_copy(k, self.dest(i)).wait_recv()
        starts = (i == 0) | (i == 2)

        @pl.when(starts)
        def _():
            self.out[k, i] = self.chip_sum(k, i).astype(BF16)

        @pl.when(jnp.logical_not(starts))
        def _():
            self.ring_copy(k, i, i).wait_recv()
            self.out[k, i] = (self.chip_sum(k, i) + self.box[k, i].astype(F32)).astype(BF16)

        self.ring_copy(k, i, jnp.where(i == 0, 1, i + 2)).start()

    def total(self, k):
        self.sib_copy(k, self.p.z).wait_recv()
        self.ring_copy(k, 0, 7).wait_recv()
        self.ring_copy(k, 0, 8).wait_recv()
        return self.chip_sum(k, jnp.int32(7)) + self.box[k, 7].astype(F32) + self.box[k, 8].astype(F32)

    def drain(self):
        def body(i, _):
            for k in range(2):
                self.ring_copy(k, i, i).wait_send()
                self.sib_copy(k, i).wait_send()
            return 0

        lax.fori_loop(0, CHIPS - 1, body, 0)
        for k in range(2):
            self.sib_copy(k, CHIPS - 1).wait_send()


def kernel(names, *refs):
    r = types.SimpleNamespace(**dict(zip(names, refs, strict=True)))
    p = Place()
    z, core = p.z, p.core
    scale = 1.0 / HEAD_DIM**0.5
    width = r.wkv.shape[2]
    heads = width // HEAD_DIM
    model = r.wout.shape[1]
    enc_width = r.wkv.shape[1]
    half_model = model // 2
    half_rows = NLEN // 2
    x, y = p.seq // 4, lax.rem(p.seq, 4)

    loads = []
    for j, (src, dst) in enumerate(
        (
            (r.nbr_in, r.nbr_raw),
            (r.wq_in, r.wq_all.at[z]),
            (r.wo_in, r.wo_all.at[z]),
            (r.tok_in.at[:, pl.ds(0, half_model)], r.tok_all.at[0, p.me]),
            (r.tok_in.at[:, pl.ds(half_model, half_model)], r.tok_all.at[1, p.me]),
            (r.dec_in, r.wdec),
            (r.wkv_in, r.wkv_raw),
            (r.wout_in, r.wout),
        )
    ):
        c = pltpu.make_async_copy(src, dst, r.load_sems.at[j])
        c.start()
        loads.append(c)
    load_nbr, load_q, load_o, load_tok0, load_tok1, load_dec, load_kv, load_out = loads

    def to_x(shift):
        return {"seq": 4 * lax.rem(x + shift + 4, 4) + y}

    def to_y(shift):
        return {"seq": 4 * x + lax.rem(y + shift + 4, 4)}

    ahead = lax.rem(p.seq + 1, p.n_seq)
    behind = lax.rem(p.seq + p.n_seq - 1, p.n_seq)
    partners = [p.on(z + h) for h in range(1, CHIPS)]
    partners += [{"nbr": p.sibling}, to_x(1), to_x(-1), to_y(1), to_y(-1), {"seq": ahead}, {"seq": behind}]
    barrier = pltpu.get_barrier_semaphore()
    for who in partners:
        pl.semaphore_signal(barrier, inc=1, device_id=who, device_id_type=MESH)
    load_nbr.wait()
    r.nbr32[...] = r.nbr_raw[...].astype(F32)
    for c in range(CHIPS):
        pair = [r.nbr32[lax.rem(r.table[k, c], r.nbr32.shape[0])] for k in range(2)]
        r.nbr_send[c] = jnp.concatenate(pair, axis=0).astype(BF16)
    r.nbr_all[z, core] = r.nbr_send[z]
    for c in (load_q, load_o, load_tok0, load_tok1):
        c.wait()
    pl.semaphore_wait(barrier, len(partners))

    def query_piece(chip, a):
        rows = pl.ds(pl.multiple_of(224 * y + 112 * (a // 2), 16), 112)
        return r.wq_all.at[chip, rows, pl.ds(pl.multiple_of(128 * lax.rem(a, 2), 128), 128)]

    def query_slab(chip, b):
        return r.wq_all.at[chip, pl.ds(pl.multiple_of(224 * b, 16), 224)]

    def out_piece(chip, a):
        return r.wo_all.at[chip, pl.ds(pl.multiple_of(64 * x + 16 * a, 16), 16)]

    def out_slab(chip, b):
        return r.wo_all.at[chip, pl.ds(pl.multiple_of(64 * b, 16), 64)]

    def stream(name, k, ref, sibling=True):
        sems = [getattr(r, name + end).at[k] for end in ("_f", "_r", "_s")[: 2 + sibling]]
        return Gather(p, ref, *sems)

    tok, enc = ([stream(name, k, getattr(r, name + "_all").at[k].at.__getitem__) for k in range(2)] for name in ("tok", "enc"))
    weights_z = [
        stream("wz", 0, lambda slot: query_piece(slot // 2, x), False),
        stream("wz", 1, lambda slot: out_piece(slot // 2, y), False),
    ]
    spread_sems = [getattr(r, "x" + c) for c in "abcdefgh"]
    weights_xy = [
        Spread(p, query_piece, query_slab, (x, to_x), (y, to_y), [s.at[0] for s in spread_sems]),
        Spread(p, out_piece, out_slab, (y, to_y), (x, to_x), [s.at[1] for s in spread_sems]),
    ]

    def weights(what, *items):
        for i in items:
            for w in weights_xy:
                getattr(w, what)(i)

    def weights_step(h):
        for w in weights_z:
            w.step(h)

    def remote(src, dst, target, send, recv):
        return pltpu.make_async_remote_copy(
            src_ref=src, dst_ref=dst, send_sem=send, recv_sem=recv, device_id=target, device_id_type=MESH
        )

    def halo(src, dst, target, j):
        return remote(src, dst, {"seq": target}, r.halo_sems.at[2 * j], r.halo_sems.at[2 * j + 1])

    send_q = halo(r.hq, r.hq_got, behind, 0)
    send_a = halo(r.ha, r.ha_got, ahead, 1)

    def nbr_copy(h):
        return remote(
            r.nbr_send.at[wrap(z + h)], r.nbr_all.at[z, core], p.on(z + h), r.nbr_sems.at[0, h], r.nbr_sems.at[1, z]
        )

    def nbr_arrived(h):
        chip = wrap(z + h)
        remote(
            r.nbr_send.at[0], r.nbr_all.at[chip, core], p.on(chip), r.nbr_sems.at[0, 0], r.nbr_sems.at[1, chip]
        ).wait_recv()

    nbr_sib = remote(
        r.nbr_all.at[:, core], r.nbr_all.at[:, core], {"nbr": p.sibling}, r.pair_sems.at[0], r.pair_sems.at[1]
    )
    nbr_sib_in = remote(
        r.nbr_all.at[:, 1 - core], r.nbr_all.at[:, 1 - core], {"nbr": p.sibling}, r.pair_sems.at[0], r.pair_sems.at[1]
    )

    def cond_copy(j, h):
        return remote(
            r.cond.at[j, wrap(z + h)], r.cond_got.at[z, j], p.on(z + h), r.cond_s.at[j, h], r.cond_r.at[j, z]
        )

    def cond_arrived(j, chip):
        remote(
            r.cond.at[j, 0], r.cond_got.at[chip, j], p.on(chip), r.cond_s.at[j, 0], r.cond_r.at[j, chip]
        ).wait_recv()

    order = (1, -1, 2, -2, 3, -3, 4)

    def project(j):
        x0, x1 = (r.tok_all[k].reshape(CHIPS * GROUP, half_model) for k in range(2))
        return dot(x0, r.wdec[j, pl.ds(0, half_model)]) + dot(x1, r.wdec[j, pl.ds(half_model, half_model)])

    def make_cond(*shifts):
        chips = [wrap(z + h) for h in shifts]
        for t in tok:
            for c in chips:
                t.from_sibling(c)
        x = [
            jnp.concatenate([r.tok_all[k, pl.ds(2 * c, 2)].reshape(GROUP, half_model) for c in chips], axis=0)
            for k in range(2)
        ]
        for j in range(2):
            y = sum(dot(x[k], r.wdec[1 + j, pl.ds(k * half_model, half_model)]) for k in range(2)).astype(BF16)
            for n, (h, c) in enumerate(zip(shifts, chips, strict=True)):
                part = y[GROUP * n : GROUP * (n + 1)]
                if h == 0:
                    r.cond_got[z, j] = part
                else:
                    r.cond[j, c] = part
                    cond_copy(j, h % CHIPS).start()

    def encode(*items):
        chips = [p.nth(i) for i in items]
        for i, chip in zip(items, chips, strict=True):
            if i > 0:
                for j in range(2):
                    cond_arrived(j, chip)
                for w in weights_xy:
                    w.ready(i)
        rows = r.nbr_all[...].reshape(2 * NLEN, enc_width)
        term = 0.0
        for chip in chips:
            queries = dot(rows, r.wq_all[chip]).astype(BF16)
            per_head = []
            for h in range(heads):
                cols = slice(HEAD_DIM * h, HEAD_DIM * (h + 1))
                shares = softmax(dot_t(queries[:, cols], r.cond_got[chip, 0, :, cols]) * scale)
                per_head.append(dot(shares, r.cond_got[chip, 1, :, cols]).astype(BF16))
            term += dot(jnp.concatenate(per_head, axis=1), r.wo_all[chip])
        if 0 in items:
            r.enc_sum[...] = term
        else:
            r.enc_sum[...] += term

    def of_slot(rows, slot):
        rows = rows.reshape(16, 2, 8, enc_width)
        return jnp.where(slot == 0, rows[:, 0], rows[:, 1]).reshape(NLEN, enc_width)

    def sum_copy(k):
        sems = r.pair_sems.at[2 + 2 * k], r.pair_sems.at[3 + 2 * k]
        return remote(r.sum_out.at[k], r.sum_got.at[k], {"nbr": p.sibling}, *sems)


    def split_kv():
        step = 128

        def body(i, _):
            mine = pl.ds(pl.multiple_of(i * step, step), step)
            both = r.wkv_raw[mine].astype(F32)
            r.wkv[0, mine] = both[:, 0].astype(BF16)
            r.wkv[1, mine] = both[:, 1].astype(BF16)
            return 0

        lax.fori_loop(0, enc_width // step, body, 0)

    def attend(*shifts):
        groups = [wrap(z + h) for h in shifts]
        for h in shifts:
            for k in range(2):
                enc[k].from_sibling(z + h)
        key = lax.broadcasted_iota(jnp.int32, (GROUP, 2 * NLEN), 1)
        slot = lax.rem(key // half_rows, 2)
        got = []
        for g in groups:
            rows = r.enc_all[:, pl.ds(2 * g, 2)].reshape(2 * NLEN, enc_width)
            keys, values = (dot(rows, r.wkv[j]).astype(BF16) for j in range(2))
            queries = r.qpad[pl.ds(pl.multiple_of(GROUP * (g + 1), GROUP), GROUP), :]
            own = (lax.broadcasted_iota(jnp.int32, queries.shape, 0) == 0) | (g != CHIPS - 1)
            queries = jnp.where(own, queries, r.hq_got[...].astype(F32)).astype(BF16)
            live = slot < r.counts[p.seq * CHIPS + g]
            per_head = []
            for h in range(heads):
                cols = slice(HEAD_DIM * h, HEAD_DIM * (h + 1))
                scores = jnp.where(live, dot_t(queries[:, cols], keys[:, cols]) * scale, -1e30)
                per_head.append(dot(softmax(scores), values[:, cols]))
            got.append(jnp.concatenate(per_head, axis=1).astype(BF16))
        for g, rows in zip(groups, got, strict=True):
            r.att[pl.ds(pl.multiple_of(GROUP * (g + 1), GROUP), GROUP), :] = rows.astype(F32)
        for g in groups:

            @pl.when(g == CHIPS - 1)
            def _():
                r.ha[...] = r.att[pl.ds(GROUP * CHIPS, GROUP), :].astype(BF16)
                send_a.start()

    out_sum = Reduce(p, r.opart, r.osib, r.obox, r.oout, (r.o0, r.o1, r.o2, r.o3))
    half = GROUP // 2
    block = 512

    def make_out(c):
        @pl.when(c == 0)
        def _():
            send_a.wait_recv()
            begins = lax.rem(p.seq * (GROUP * CHIPS), SEQ_LEN) == 0
            r.att[pl.ds(0, GROUP), :] = jnp.where(begins, 0.0, r.ha_got[...].astype(F32))

        wide = r.att[pl.ds(pl.multiple_of(GROUP * c, GROUP), GROUP + 8), :]
        rows = wide[1 : GROUP + 1].astype(BF16)

        for k in range(2):

            def body(j, _, k=k):
                cols = pl.ds(pl.multiple_of(j * block, block), block)
                weight = r.wout[:, pl.ds(pl.multiple_of(k * half_model + j * block, block), block)]
                y = dot(rows, weight).astype(BF16)
                r.opart[k, c, 0, :, cols] = y[:half]
                r.opart[k, c, 1, :, cols] = y[half:]
                return 0

            lax.fori_loop(0, half_model // block, body, 0)
            out_sum.sib_copy(k, c).start()

    def make_outs(chips):
        for c in chips:
            make_out(wrap(c))

    for g in (*weights_z, *tok):
        g.own()
    weights_step(1)
    weights("pieces_out", 1, 2)
    load_kv.wait()
    split_kv()
    for h in order:
        nbr_copy(h % CHIPS).start()
    weights_step(2)
    weights("pieces_out", 3, 4)
    weights("pieces_on", 1, 2)
    tok[0].step(1)
    tok[1].step(1)
    weights_step(3)
    weights("pieces_out", 5, 6)
    weights("slabs_out", 1, 2)
    weights("pieces_on", 3, 4)
    weights_step(4)
    weights("pieces_out", 7)
    weights("slabs_out", 3)
    weights("pieces_on", 5, 6)
    load_dec.wait()
    make_cond(0)
    tok[0].step(2)
    tok[1].step(2)
    weights("slabs_on", 1)
    weights("slabs_out", 4)
    weights("pieces_on", 7)
    weights("slabs_on", 2)
    weights("slabs_out", 5)
    for h in order:
        nbr_arrived(h)
    nbr_sib.start()
    make_cond(1, -1)
    nbr_sib_in.wait_recv()
    encode(0)
    tok[0].step(3)
    tok[1].step(3)
    weights("slabs_on", 3)
    weights("slabs_out", 6)
    make_cond(2, -2)
    weights("slabs_on", 4)
    weights("slabs_out", 7)
    encode(1, 2)
    tok[0].step(4)
    tok[1].step(4)
    make_cond(3, -3)
    make_cond(4)
    weights("slabs_on", 5)
    weights("slabs_on", 6)
    encode(3, 4)
    weights("slabs_on", 7)
    encode(5, 6)
    encode(7)

    theirs = of_slot(r.enc_sum[...], 1 - core)
    for k in range(2):
        r.sum_out[k] = theirs[half_rows * k : half_rows * (k + 1)].astype(BF16)
        sum_copy(k).start()
    mine = of_slot(r.nbr_all[...].astype(F32).reshape(2 * NLEN, enc_width), core) + of_slot(r.enc_sum[...], core)
    gain = r.gain[...].reshape(1, enc_width)
    for k in range(2):
        sum_copy(k).wait_recv()
        rows = slice(half_rows * k, half_rows * (k + 1))
        combined = mine[rows] + r.sum_got[k].astype(F32)
        factor = lax.rsqrt(jnp.mean(combined * combined, axis=-1, keepdims=True) + 1e-06)
        encoded = (combined * factor * gain).astype(BF16)
        r.enc_all[k, p.me] = encoded
        enc[k].own()
        r.enc_ref[rows] = encoded
    r.qpad[pl.ds(1, CHIPS * GROUP), :] = project(0).astype(BF16).astype(F32)
    r.hq[...] = r.qpad[pl.ds(0, GROUP), :].astype(BF16)
    send_q.start()
    load_out.wait()
    def enc_step(h):
        for k in range(2):
            enc[k].step(h)

    enc_step(1)
    send_q.wait_recv()
    attend(0)
    enc_step(2)
    attend(1, -1)
    enc_step(3)
    attend(2, -2)
    attend(3, -3)
    enc_step(4)
    attend(4)
    make_outs((z + 4,))

    def out_items(*items):
        for i in items:
            for k in range(2):
                out_sum.item(k, jnp.int32(i))

    out_items(0)
    make_outs((z + 3, z - 3))
    out_items(2)
    out_items(1)
    make_outs((z + 2, z - 2))
    out_items(4)
    out_items(3)
    make_outs((z - 1, z + 1))
    out_items(6, 5)
    make_outs((z,))
    for k in range(2):
        r.out_ref[:, pl.ds(k * half_model, half_model)] = out_sum.total(k).astype(BF16)

    for g in (*tok, *enc, *weights_z, *weights_xy):
        g.drain()
    out_sum.drain()
    for h in range(1, CHIPS):
        nbr_copy(h).wait_send()
        for j in range(2):
            cond_copy(j, h).wait_send()
    for c in (nbr_sib, sum_copy(0), sum_copy(1), send_q, send_a):
        c.wait_send()


def hand_out(out_in, enc_in, out_ref, enc_ref, sems):
    copies = [
        pltpu.make_async_copy(out_in, out_ref, sems.at[0]),
        pltpu.make_async_copy(enc_in, enc_ref, sems.at[1]),
    ]
    for c in copies:
        c.start()
    for c in copies:
        c.wait()


def local(
    tokens, nbr_embed, neighbour_table, valid_counts, dec_proj, enc_query, enc_out, enc_gain, nbr_proj, out_proj
):
    rows, model = tokens.shape
    nbrs, piece, enc_width = nbr_embed.shape
    width = enc_query.shape[1]
    block = 2 * piece
    sub = NLEN // 2
    padded = GROUP * (CHIPS + 1) + 8
    dma = pltpu.SemaphoreType.DMA
    half = (rows, model // 2)
    scratch = {
        "tok_all": pltpu.VMEM((2, 16, *half), BF16),
        "enc_all": pltpu.VMEM((2, 16, sub, enc_width), BF16),
        "nbr_all": pltpu.VMEM((CHIPS, 2, block, enc_width), BF16),
        "nbr_send": pltpu.VMEM((CHIPS, block, enc_width), BF16),
        "nbr_raw": pltpu.VMEM((nbrs, piece, enc_width), BF16),
        "nbr32": pltpu.VMEM((nbrs, piece, enc_width), F32),
        "wdec": pltpu.VMEM((3, model, width), BF16),
        "wq_all": pltpu.VMEM((CHIPS, enc_width, width), BF16),
        "wo_all": pltpu.VMEM((CHIPS, width, enc_width), BF16),
        "wkv_raw": pltpu.VMEM((enc_width, 2, width), BF16),
        "wkv": pltpu.VMEM((2, enc_width, width), BF16),
        "wout": pltpu.VMEM((width, model), BF16),
        "qpad": pltpu.VMEM((padded, width), F32),
        "cond": pltpu.VMEM((2, CHIPS, GROUP, width), BF16),
        "cond_got": pltpu.VMEM((CHIPS, 2, GROUP, width), BF16),
        "enc_sum": pltpu.VMEM((2 * NLEN, enc_width), F32),
        "sum_out": pltpu.VMEM((2, sub, enc_width), BF16),
        "sum_got": pltpu.VMEM((2, sub, enc_width), BF16),
        "att": pltpu.VMEM((padded, width), F32),
        "opart": pltpu.VMEM((2, CHIPS, 2, *half), BF16),
        "osib": pltpu.VMEM((2, CHIPS, *half), BF16),
        "obox": pltpu.VMEM((2, CHIPS + 1, *half), BF16),
        "oout": pltpu.VMEM((2, CHIPS - 1, *half), BF16),
        **{name: pltpu.VMEM((GROUP, width), BF16) for name in ("hq", "hq_got", "ha", "ha_got")},
        "load_sems": dma((8,)),
        "halo_sems": dma((4,)),
        "nbr_sems": dma((2, CHIPS)),
        "pair_sems": dma((6,)),
        "cond_s": dma((2, CHIPS)),
        "cond_r": dma((2, CHIPS)),
        **{f"{name}_{x}": dma((2, n)) for name in ("tok", "enc", "wz") for x, n in (("f", 7), ("s", 8), ("r", 16))},
        **{f"x{c}": dma((2, CHIPS, 2)) if c in "abef" else dma((2, CHIPS)) for c in "abcdefgh"},
        **{f"o{j}": dma((2, n)) for j, n in enumerate((8, 8, 7, 9))},
    }
    inputs = {
        "tok_in": (tokens, pl.ANY),
        "nbr_in": (nbr_embed, pl.ANY),
        "table": (neighbour_table.T, pltpu.SMEM),
        "counts": (valid_counts, pltpu.SMEM),
        "dec_in": (jnp.transpose(dec_proj, (1, 0, 2)), pl.ANY),
        "wq_in": (enc_query, pl.ANY),
        "wo_in": (enc_out, pl.ANY),
        "gain": (enc_gain, pltpu.VMEM),
        "wkv_in": (nbr_proj, pl.ANY),
        "wout_in": (out_proj, pl.ANY),
    }
    vmem = pl.BlockSpec(memory_space=pltpu.VMEM)
    names = (*inputs, "out_ref", "enc_ref", *scratch)
    results = pl.pallas_call(
        functools.partial(kernel, names),
        out_shape=(
            jax.ShapeDtypeStruct((rows, model), BF16),
            jax.ShapeDtypeStruct((NLEN, enc_width), BF16),
        ),
        in_specs=[pl.BlockSpec(memory_space=space) for _, space in inputs.values()],
        out_specs=(vmem, vmem),
        scratch_shapes=list(scratch.values()),
        compiler_params=pltpu.CompilerParams(
            collective_id=0, has_side_effects=True, vmem_limit_bytes=60 * 2**20
        ),
        name="retrieval",
    )(*(array for array, _ in inputs.values()))
    any_space = pl.BlockSpec(memory_space=pl.ANY)
    return pl.pallas_call(
        hand_out,
        out_shape=tuple(jax.ShapeDtypeStruct(a.shape, a.dtype) for a in results),
        in_specs=[vmem] * 2,
        out_specs=(any_space,) * 2,
        scratch_shapes=[dma((2,))],
        name="hand_out",
    )(*results)


def solution(mesh):
    return jax.shard_map(
        local,
        mesh=mesh,
        in_specs=(
            P(("seq", "nbr"), None),
            P("seq", "nbr", None),
            P("seq", None),
            P(),
            P(None, None, "nbr"),
            P(None, "nbr"),
            P("nbr", None),
            P(),
            P(None, None, "nbr"),
            P("nbr", None),
        ),
        out_specs=(P(("seq", "nbr"), None), P(("seq", "nbr"), None)),
        check_vma=False,
    )
```

```python
import functools
import types

import jax
import jax.numpy as jnp
from jax import lax
from jax.experimental import pallas as pl
from jax.experimental.pallas import tpu as pltpu
from jax.sharding import PartitionSpec as P

HEAD_DIM = 128
GROUP = 64
NLEN = 128
SEQ_LEN = 2048
CHIPS = 8
F32 = jnp.float32
BF16 = jnp.bfloat16
MESH = pl.DeviceIdType.MESH


def dot(a, b):
    return jnp.dot(a, b, preferred_element_type=F32)


def dot_t(a, b):
    return lax.dot_general(a, b, (((1,), (1,)), ((), ())), preferred_element_type=F32)


def softmax(scores):
    peak = jnp.max(scores, axis=-1, keepdims=True)
    raised = jnp.exp(scores - peak)
    return (raised * (1.0 / jnp.sum(raised, axis=-1, keepdims=True))).astype(BF16)


def wrap(x):
    return lax.rem(x + 2 * CHIPS, CHIPS)


class Place:
    def __init__(self):
        self.seq = lax.axis_index("seq")
        self.n_seq = lax.axis_size("seq")
        me = lax.axis_index("nbr")
        self.me = me
        self.z = me // 2
        self.core = lax.rem(me, 2)
        self.d = 1 - 2 * self.core
        self.sibling = me + self.d

    def on(self, chip):
        return {"nbr": 2 * wrap(chip) + self.core}

    def nth(self, i):
        sign = jnp.where(lax.rem(i, 2) == 1, 1, -1)
        return wrap(self.z + sign * ((i + 1) // 2))


class Gather:
    def __init__(self, place, ref, forward_sems, recv_sems, sibling_sems=None):
        self.p, self.ref = place, ref
        self.fs, self.rs, self.ss = forward_sems, recv_sems, sibling_sems
        self.sent = []

    def copy(self, chip, core, target, sem):
        slot = 2 * wrap(chip) + core
        return pltpu.make_async_remote_copy(
            src_ref=self.ref(slot),
            dst_ref=self.ref(slot),
            send_sem=sem,
            recv_sem=self.rs.at[slot],
            device_id=target,
            device_id_type=MESH,
        )

    def start(self, chip, target, sem):
        c = self.copy(chip, self.p.core, target, sem)
        c.start()
        self.sent.append(c)

    def to_sibling(self, chip, i):
        if self.ss is not None:
            self.start(chip, {"nbr": self.p.sibling}, self.ss.at[i])

    def arrived(self, chip):
        self.copy(chip, self.p.core, {"nbr": self.p.sibling}, self.fs.at[0]).wait_recv()

    def from_sibling(self, chip):
        self.copy(chip, 1 - self.p.core, {"nbr": self.p.sibling}, self.fs.at[0]).wait_recv()

    def own(self):
        z = self.p.z
        self.start(z, self.p.on(z + 1), self.fs.at[0])
        self.start(z, self.p.on(z - 1), self.fs.at[1])
        self.to_sibling(z, 0)

    def step(self, h):
        z, d = self.p.z, self.p.d
        if h < 3:
            for j, sign in enumerate((1, -1)):
                self.arrived(z - sign * h)
                self.start(z - sign * h, self.p.on(z + sign), self.fs.at[2 * h + j])
                self.to_sibling(z - sign * h, 2 * h - 1 + j)
        elif h == 3:
            self.arrived(z - 3 * d)
            self.start(z - 3 * d, self.p.on(z + d), self.fs.at[6])
            self.to_sibling(z - 3 * d, 5)
            self.arrived(z + 3 * d)
            self.to_sibling(z + 3 * d, 6)
        else:
            self.arrived(z + 4)
            self.to_sibling(z + 4, 7)

    def drain(self):
        for c in self.sent:
            c.wait_send()


class Spread:
    def __init__(self, place, piece, slab, first, second, sems):
        self.p, self.piece, self.slab = place, piece, slab
        (self.a, self.to_first), (self.b, self.to_second) = first, second
        self.bs, self.br, self.cs, self.cr, self.ds, self.dr, self.es, self.er = sems
        self.sent = []

    def copy(self, ref, target, send, recv):
        return pltpu.make_async_remote_copy(
            src_ref=ref, dst_ref=ref, send_sem=send, recv_sem=recv, device_id=target, device_id_type=MESH
        )

    def start(self, *copy):
        c = self.copy(*copy)
        c.start()
        self.sent.append(c)

    def send_both(self, i, ref, to, send, recv):
        for j, sign in enumerate((1, -1)):
            self.start(ref, to(sign), send.at[i, j], recv.at[i, j])

    def pass_on(self, i, ref, to, arrived, send, recv):
        for j, sign in enumerate((1, -1)):
            self.copy(ref(-sign), to(sign), send.at[i], arrived.at[i, j]).wait_recv()
        sign = 1 if i % 2 else -1
        self.start(ref(-sign), to(sign), send.at[i], recv.at[i])

    def piece_at(self, i, shift):
        return self.piece(self.p.nth(i), lax.rem(self.a + shift + 4, 4))

    def slab_at(self, i, shift):
        return self.slab(self.p.nth(i), lax.rem(self.b + shift + 4, 4))

    def pieces_out(self, i):
        self.send_both(i, self.piece_at(i, 0), self.to_first, self.bs, self.br)

    def pieces_on(self, i):
        self.pass_on(i, functools.partial(self.piece_at, i), self.to_first, self.br, self.cs, self.cr)

    def slabs_out(self, i):
        self.copy(self.piece_at(i, 2), self.to_first(1), self.cs.at[i], self.cr.at[i]).wait_recv()
        self.send_both(i, self.slab_at(i, 0), self.to_second, self.ds, self.dr)

    def slabs_on(self, i):
        self.pass_on(i, functools.partial(self.slab_at, i), self.to_second, self.dr, self.es, self.er)

    def ready(self, i):
        self.copy(self.slab_at(i, 2), self.to_second(1), self.es.at[i], self.er.at[i]).wait_recv()

    def drain(self):
        for c in self.sent:
            c.wait_send()


class Reduce:
    def __init__(self, place, part, from_sib, box, out, sems):
        self.p, self.part, self.from_sib, self.box, self.out = place, part, from_sib, box, out
        self.sib_send, self.sib_recv, self.send, self.recv = sems

    def sign(self, i):
        return jnp.where((i == 0) | (lax.rem(i, 2) == 1), self.p.d, -self.p.d)

    def dest(self, i):
        return wrap(self.p.z + self.sign(i) * (4 - (i + 1) // 2))

    def sib_copy(self, k, c):
        return pltpu.make_async_remote_copy(
            src_ref=self.part.at[k, c, 1 - self.p.core],
            dst_ref=self.from_sib.at[k, c],
            send_sem=self.sib_send.at[k, c],
            recv_sem=self.sib_recv.at[k, c],
            device_id={"nbr": self.p.sibling},
            device_id_type=MESH,
        )

    def ring_copy(self, k, i, land):
        return pltpu.make_async_remote_copy(
            src_ref=self.out.at[k, i],
            dst_ref=self.box.at[k, land],
            send_sem=self.send.at[k, i],
            recv_sem=self.recv.at[k, land],
            device_id=self.p.on(self.p.z + self.sign(i)),
            device_id_type=MESH,
        )

    def chip_sum(self, k, i):
        c = self.dest(i)
        return self.part[k, c, self.p.core].astype(F32) + self.from_sib[k, c].astype(F32)

    def item(self, k, i):
        self.sib_copy(k, self.dest(i)).wait_recv()
        starts = (i == 0) | (i == 2)

        @pl.when(starts)
        def _():
            self.out[k, i] = self.chip_sum(k, i).astype(BF16)

        @pl.when(jnp.logical_not(starts))
        def _():
            self.ring_copy(k, i, i).wait_recv()
            self.out[k, i] = (self.chip_sum(k, i) + self.box[k, i].astype(F32)).astype(BF16)

        self.ring_copy(k, i, jnp.where(i == 0, 1, i + 2)).start()

    def total(self, k):
        self.sib_copy(k, self.p.z).wait_recv()
        self.ring_copy(k, 0, 7).wait_recv()
        self.ring_copy(k, 0, 8).wait_recv()
        return self.chip_sum(k, jnp.int32(7)) + self.box[k, 7].astype(F32) + self.box[k, 8].astype(F32)

    def drain(self):
        def body(i, _):
            for k in range(2):
                self.ring_copy(k, i, i).wait_send()
                self.sib_copy(k, i).wait_send()
            return 0

        lax.fori_loop(0, CHIPS - 1, body, 0)
        for k in range(2):
            self.sib_copy(k, CHIPS - 1).wait_send()


def kernel(names, *refs):
    r = types.SimpleNamespace(**dict(zip(names, refs, strict=True)))
    p = Place()
    z, core = p.z, p.core
    scale = 1.0 / HEAD_DIM**0.5
    width = r.wkv.shape[2]
    heads = width // HEAD_DIM
    model = r.wout.shape[1]
    enc_width = r.wkv.shape[1]
    half_model = model // 2
    half_rows = NLEN // 2
    x, y = p.seq // 4, lax.rem(p.seq, 4)

    loads = []
    for j, (src, dst) in enumerate(
        (
            (r.nbr_in, r.nbr_raw),
            (r.wq_in, r.wq_all.at[z]),
            (r.wo_in, r.wo_all.at[z]),
            (r.tok_in.at[:, pl.ds(0, half_model)], r.tok_all.at[0, p.me]),
            (r.tok_in.at[:, pl.ds(half_model, half_model)], r.tok_all.at[1, p.me]),
            (r.dec_in, r.wdec),
            (r.wkv_in, r.wkv_raw),
            (r.wout_in, r.wout),
        )
    ):
        c = pltpu.make_async_copy(src, dst, r.load_sems.at[j])
        c.start()
        loads.append(c)
    load_nbr, load_q, load_o, load_tok0, load_tok1, load_dec, load_kv, load_out = loads

    def to_x(shift):
        return {"seq": 4 * lax.rem(x + shift + 4, 4) + y}

    def to_y(shift):
        return {"seq": 4 * x + lax.rem(y + shift + 4, 4)}

    ahead = lax.rem(p.seq + 1, p.n_seq)
    behind = lax.rem(p.seq + p.n_seq - 1, p.n_seq)
    partners = [p.on(z + h) for h in range(1, CHIPS)]
    partners += [{"nbr": p.sibling}, to_x(1), to_x(-1), to_y(1), to_y(-1), {"seq": ahead}, {"seq": behind}]
    barrier = pltpu.get_barrier_semaphore()
    for who in partners:
        pl.semaphore_signal(barrier, inc=1, device_id=who, device_id_type=MESH)
    load_nbr.wait()
    r.nbr32[...] = r.nbr_raw[...].astype(F32)
    for c in range(CHIPS):
        pair = [r.nbr32[lax.rem(r.table[k, c], r.nbr32.shape[0])] for k in range(2)]
        r.nbr_send[c] = jnp.concatenate(pair, axis=0).astype(BF16)
    r.nbr_all[z, core] = r.nbr_send[z]
    for c in (load_q, load_o, load_tok0, load_tok1):
        c.wait()
    pl.semaphore_wait(barrier, len(partners))

    def query_piece(chip, a):
        rows = pl.ds(pl.multiple_of(224 * y + 112 * (a // 2), 16), 112)
        return r.wq_all.at[chip, rows, pl.ds(pl.multiple_of(128 * lax.rem(a, 2), 128), 128)]

    def query_slab(chip, b):
        return r.wq_all.at[chip, pl.ds(pl.multiple_of(224 * b, 16), 224)]

    def out_piece(chip, a):
        return r.wo_all.at[chip, pl.ds(pl.multiple_of(64 * x + 16 * a, 16), 16)]

    def out_slab(chip, b):
        return r.wo_all.at[chip, pl.ds(pl.multiple_of(64 * b, 16), 64)]

    def stream(name, k, ref, sibling=True):
        sems = [getattr(r, name + end).at[k] for end in ("_f", "_r", "_s")[: 2 + sibling]]
        return Gather(p, ref, *sems)

    tok, enc = ([stream(name, k, getattr(r, name + "_all").at[k].at.__getitem__) for k in range(2)] for name in ("tok", "enc"))
    weights_z = [
        stream("wz", 0, lambda slot: query_piece(slot // 2, x), False),
        stream("wz", 1, lambda slot: out_piece(slot // 2, y), False),
    ]
    spread_sems = [getattr(r, "x" + c) for c in "abcdefgh"]
    weights_xy = [
        Spread(p, query_piece, query_slab, (x, to_x), (y, to_y), [s.at[0] for s in spread_sems]),
        Spread(p, out_piece, out_slab, (y, to_y), (x, to_x), [s.at[1] for s in spread_sems]),
    ]

    def weights(what, *items):
        for i in items:
            for w in weights_xy:
                getattr(w, what)(i)

    def weights_step(h):
        for w in weights_z:
            w.step(h)

    def remote(src, dst, target, send, recv):
        return pltpu.make_async_remote_copy(
            src_ref=src, dst_ref=dst, send_sem=send, recv_sem=recv, device_id=target, device_id_type=MESH
        )

    def halo(src, dst, target, j):
        return remote(src, dst, {"seq": target}, r.halo_sems.at[2 * j], r.halo_sems.at[2 * j + 1])

    send_q = halo(r.hq, r.hq_got, behind, 0)
    send_a = halo(r.ha, r.ha_got, ahead, 1)

    def nbr_copy(h):
        return remote(
            r.nbr_send.at[wrap(z + h)], r.nbr_all.at[z, core], p.on(z + h), r.nbr_sems.at[0, h], r.nbr_sems.at[1, z]
        )

    def nbr_arrived(h):
        chip = wrap(z + h)
        remote(
            r.nbr_send.at[0], r.nbr_all.at[chip, core], p.on(chip), r.nbr_sems.at[0, 0], r.nbr_sems.at[1, chip]
        ).wait_recv()

    nbr_sib = remote(
        r.nbr_all.at[:, core], r.nbr_all.at[:, core], {"nbr": p.sibling}, r.pair_sems.at[0], r.pair_sems.at[1]
    )
    nbr_sib_in = remote(
        r.nbr_all.at[:, 1 - core], r.nbr_all.at[:, 1 - core], {"nbr": p.sibling}, r.pair_sems.at[0], r.pair_sems.at[1]
    )

    def cond_copy(j, h):
        return remote(
            r.cond.at[j, wrap(z + h)], r.cond_got.at[z, j], p.on(z + h), r.cond_s.at[j, h], r.cond_r.at[j, z]
        )

    def cond_arrived(j, chip):
        remote(
            r.cond.at[j, 0], r.cond_got.at[chip, j], p.on(chip), r.cond_s.at[j, 0], r.cond_r.at[j, chip]
        ).wait_recv()

    order = (1, -1, 2, -2, 3, -3, 4)

    def project(j):
        x0, x1 = (r.tok_all[k].reshape(CHIPS * GROUP, half_model) for k in range(2))
        return dot(x0, r.wdec[j, pl.ds(0, half_model)]) + dot(x1, r.wdec[j, pl.ds(half_model, half_model)])

    def make_cond(*shifts):
        chips = [wrap(z + h) for h in shifts]
        for t in tok:
            for c in chips:
                t.from_sibling(c)
        x = [
            jnp.concatenate([r.tok_all[k, pl.ds(2 * c, 2)].reshape(GROUP, half_model) for c in chips], axis=0)
            for k in range(2)
        ]
        for j in range(2):
            y = sum(dot(x[k], r.wdec[1 + j, pl.ds(k * half_model, half_model)]) for k in range(2)).astype(BF16)
            for n, (h, c) in enumerate(zip(shifts, chips, strict=True)):
                part = y[GROUP * n : GROUP * (n + 1)]
                if h == 0:
                    r.cond_got[z, j] = part
                else:
                    r.cond[j, c] = part
                    cond_copy(j, h % CHIPS).start()

    def encode(*items):
        chips = [p.nth(i) for i in items]
        for i, chip in zip(items, chips, strict=True):
            if i > 0:
                for j in range(2):
                    cond_arrived(j, chip)
                for w in weights_xy:
                    w.ready(i)
        rows = r.nbr_all[...].reshape(2 * NLEN, enc_width)
        term = 0.0
        for chip in chips:
            queries = dot(rows, r.wq_all[chip]).astype(BF16)
            per_head = []
            for h in range(heads):
                cols = slice(HEAD_DIM * h, HEAD_DIM * (h + 1))
                shares = softmax(dot_t(queries[:, cols], r.cond_got[chip, 0, :, cols]) * scale)
                per_head.append(dot(shares, r.cond_got[chip, 1, :, cols]).astype(BF16))
            term += dot(jnp.concatenate(per_head, axis=1), r.wo_all[chip])
        if 0 in items:
            r.enc_sum[...] = term
        else:
            r.enc_sum[...] += term

    def of_slot(rows, slot):
        rows = rows.reshape(16, 2, 8, enc_width)
        return jnp.where(slot == 0, rows[:, 0], rows[:, 1]).reshape(NLEN, enc_width)

    def sum_copy(k):
        sems = r.pair_sems.at[2 + 2 * k], r.pair_sems.at[3 + 2 * k]
        return remote(r.sum_out.at[k], r.sum_got.at[k], {"nbr": p.sibling}, *sems)


    def split_kv():
        step = 128

        def body(i, _):
            mine = pl.ds(pl.multiple_of(i * step, step), step)
            both = r.wkv_raw[mine].astype(F32)
            r.wkv[0, mine] = both[:, 0].astype(BF16)
            r.wkv[1, mine] = both[:, 1].astype(BF16)
            return 0

        lax.fori_loop(0, enc_width // step, body, 0)

    def attend(*shifts):
        groups = [wrap(z + h) for h in shifts]
        for h in shifts:
            for k in range(2):
                enc[k].from_sibling(z + h)
        key = lax.broadcasted_iota(jnp.int32, (GROUP, 2 * NLEN), 1)
        slot = lax.rem(key // half_rows, 2)
        got = []
        for g in groups:
            rows = r.enc_all[:, pl.ds(2 * g, 2)].reshape(2 * NLEN, enc_width)
            keys, values = (dot(rows, r.wkv[j]).astype(BF16) for j in range(2))
            queries = r.qpad[pl.ds(pl.multiple_of(GROUP * (g + 1), GROUP), GROUP), :]
            own = (lax.broadcasted_iota(jnp.int32, queries.shape, 0) == 0) | (g != CHIPS - 1)
            queries = jnp.where(own, queries, r.hq_got[...].astype(F32)).astype(BF16)
            live = slot < r.counts[p.seq * CHIPS + g]
            per_head = []
            for h in range(heads):
                cols = slice(HEAD_DIM * h, HEAD_DIM * (h + 1))
                scores = jnp.where(live, dot_t(queries[:, cols], keys[:, cols]) * scale, -1e30)
                per_head.append(dot(softmax(scores), values[:, cols]))
            got.append(jnp.concatenate(per_head, axis=1).astype(BF16))
        for g, rows in zip(groups, got, strict=True):
            r.att[pl.ds(pl.multiple_of(GROUP * (g + 1), GROUP), GROUP), :] = rows.astype(F32)
        for g in groups:

            @pl.when(g == CHIPS - 1)
            def _():
                r.ha[...] = r.att[pl.ds(GROUP * CHIPS, GROUP), :].astype(BF16)
                send_a.start()

    out_sum = Reduce(p, r.opart, r.osib, r.obox, r.oout, (r.o0, r.o1, r.o2, r.o3))
    half = GROUP // 2
    block = 512

    def make_out(c):
        @pl.when(c == 0)
        def _():
            send_a.wait_recv()
            begins = lax.rem(p.seq * (GROUP * CHIPS), SEQ_LEN) == 0
            r.att[pl.ds(0, GROUP), :] = jnp.where(begins, 0.0, r.ha_got[...].astype(F32))

        wide = r.att[pl.ds(pl.multiple_of(GROUP * c, GROUP), GROUP + 8), :]
        rows = wide[1 : GROUP + 1].astype(BF16)

        for k in range(2):

            def body(j, _, k=k):
                cols = pl.ds(pl.multiple_of(j * block, block), block)
                weight = r.wout[:, pl.ds(pl.multiple_of(k * half_model + j * block, block), block)]
                y = dot(rows, weight).astype(BF16)
                r.opart[k, c, 0, :, cols] = y[:half]
                r.opart[k, c, 1, :, cols] = y[half:]
                return 0

            lax.fori_loop(0, half_model // block, body, 0)
            out_sum.sib_copy(k, c).start()

    def make_outs(chips):
        for c in chips:
            make_out(wrap(c))

    for g in (*weights_z, *tok):
        g.own()
    weights_step(1)
    weights("pieces_out", 1, 2)
    load_kv.wait()
    split_kv()
    for h in order:
        nbr_copy(h % CHIPS).start()
    weights_step(2)
    weights("pieces_out", 3, 4)
    weights("pieces_on", 1, 2)
    tok[0].step(1)
    tok[1].step(1)
    weights_step(3)
    weights("pieces_out", 5, 6)
    weights("slabs_out", 1, 2)
    weights("pieces_on", 3, 4)
    weights_step(4)
    weights("pieces_out", 7)
    weights("slabs_out", 3)
    weights("pieces_on", 5, 6)
    load_dec.wait()
    make_cond(0)
    tok[0].step(2)
    tok[1].step(2)
    weights("slabs_on", 1)
    weights("slabs_out", 4)
    weights("pieces_on", 7)
    weights("slabs_on", 2)
    weights("slabs_out", 5)
    for h in order:
        nbr_arrived(h)
    nbr_sib.start()
    make_cond(1, -1)
    nbr_sib_in.wait_recv()
    encode(0)
    tok[0].step(3)
    tok[1].step(3)
    weights("slabs_on", 3)
    weights("slabs_out", 6)
    make_cond(2, -2)
    weights("slabs_on", 4)
    weights("slabs_out", 7)
    encode(1, 2)
    tok[0].step(4)
    tok[1].step(4)
    make_cond(3, -3)
    make_cond(4)
    weights("slabs_on", 5)
    weights("slabs_on", 6)
    encode(3, 4)
    weights("slabs_on", 7)
    encode(5, 6)
    encode(7)

    theirs = of_slot(r.enc_sum[...], 1 - core)
    for k in range(2):
        r.sum_out[k] = theirs[half_rows * k : half_rows * (k + 1)].astype(BF16)
        sum_copy(k).start()
    mine = of_slot(r.nbr_all[...].astype(F32).reshape(2 * NLEN, enc_width), core) + of_slot(r.enc_sum[...], core)
    gain = r.gain[...].reshape(1, enc_width)
    for k in range(2):
        sum_copy(k).wait_recv()
        rows = slice(half_rows * k, half_rows * (k + 1))
        combined = mine[rows] + r.sum_got[k].astype(F32)
        factor = lax.rsqrt(jnp.mean(combined * combined, axis=-1, keepdims=True) + 1e-06)
        encoded = (combined * factor * gain).astype(BF16)
        r.enc_all[k, p.me] = encoded
        enc[k].own()
        r.enc_ref[rows] = encoded
    r.qpad[pl.ds(1, CHIPS * GROUP), :] = project(0).astype(BF16).astype(F32)
    r.hq[...] = r.qpad[pl.ds(0, GROUP), :].astype(BF16)
    send_q.start()
    load_out.wait()
    def enc_step(h):
        for k in range(2):
            enc[k].step(h)

    enc_step(1)
    send_q.wait_recv()
    attend(0)
    enc_step(2)
    attend(1, -1)
    enc_step(3)
    attend(2, -2)
    enc_step(4)
    attend(3, -3)
    attend(4)
    make_outs((z + 4,))

    def out_items(*items):
        for i in items:
            for k in range(2):
                out_sum.item(k, jnp.int32(i))

    out_items(0)
    make_outs((z + 3, z - 3))
    out_items(2)
    out_items(1)
    make_outs((z + 2, z - 2))
    out_items(4)
    out_items(3)
    make_outs((z - 1, z + 1))
    out_items(6, 5)
    make_outs((z,))
    for k in range(2):
        r.out_ref[:, pl.ds(k * half_model, half_model)] = out_sum.total(k).astype(BF16)

    for g in (*tok, *enc, *weights_z, *weights_xy):
        g.drain()
    out_sum.drain()
    for h in range(1, CHIPS):
        nbr_copy(h).wait_send()
        for j in range(2):
            cond_copy(j, h).wait_send()
    for c in (nbr_sib, sum_copy(0), sum_copy(1), send_q, send_a):
        c.wait_send()


def hand_out(out_in, enc_in, out_ref, enc_ref, sems):
    copies = [
        pltpu.make_async_copy(out_in, out_ref, sems.at[0]),
        pltpu.make_async_copy(enc_in, enc_ref, sems.at[1]),
    ]
    for c in copies:
        c.start()
    for c in copies:
        c.wait()


def local(
    tokens, nbr_embed, neighbour_table, valid_counts, dec_proj, enc_query, enc_out, enc_gain, nbr_proj, out_proj
):
    rows, model = tokens.shape
    nbrs, piece, enc_width = nbr_embed.shape
    width = enc_query.shape[1]
    block = 2 * piece
    sub = NLEN // 2
    padded = GROUP * (CHIPS + 1) + 8
    dma = pltpu.SemaphoreType.DMA
    half = (rows, model // 2)
    scratch = {
        "tok_all": pltpu.VMEM((2, 16, *half), BF16),
        "enc_all": pltpu.VMEM((2, 16, sub, enc_width), BF16),
        "nbr_all": pltpu.VMEM((CHIPS, 2, block, enc_width), BF16),
        "nbr_send": pltpu.VMEM((CHIPS, block, enc_width), BF16),
        "nbr_raw": pltpu.VMEM((nbrs, piece, enc_width), BF16),
        "nbr32": pltpu.VMEM((nbrs, piece, enc_width), F32),
        "wdec": pltpu.VMEM((3, model, width), BF16),
        "wq_all": pltpu.VMEM((CHIPS, enc_width, width), BF16),
        "wo_all": pltpu.VMEM((CHIPS, width, enc_width), BF16),
        "wkv_raw": pltpu.VMEM((enc_width, 2, width), BF16),
        "wkv": pltpu.VMEM((2, enc_width, width), BF16),
        "wout": pltpu.VMEM((width, model), BF16),
        "qpad": pltpu.VMEM((padded, width), F32),
        "cond": pltpu.VMEM((2, CHIPS, GROUP, width), BF16),
        "cond_got": pltpu.VMEM((CHIPS, 2, GROUP, width), BF16),
        "enc_sum": pltpu.VMEM((2 * NLEN, enc_width), F32),
        "sum_out": pltpu.VMEM((2, sub, enc_width), BF16),
        "sum_got": pltpu.VMEM((2, sub, enc_width), BF16),
        "att": pltpu.VMEM((padded, width), F32),
        "opart": pltpu.VMEM((2, CHIPS, 2, *half), BF16),
        "osib": pltpu.VMEM((2, CHIPS, *half), BF16),
        "obox": pltpu.VMEM((2, CHIPS + 1, *half), BF16),
        "oout": pltpu.VMEM((2, CHIPS - 1, *half), BF16),
        **{name: pltpu.VMEM((GROUP, width), BF16) for name in ("hq", "hq_got", "ha", "ha_got")},
        "load_sems": dma((8,)),
        "halo_sems": dma((4,)),
        "nbr_sems": dma((2, CHIPS)),
        "pair_sems": dma((6,)),
        "cond_s": dma((2, CHIPS)),
        "cond_r": dma((2, CHIPS)),
        **{f"{name}_{x}": dma((2, n)) for name in ("tok", "enc", "wz") for x, n in (("f", 7), ("s", 8), ("r", 16))},
        **{f"x{c}": dma((2, CHIPS, 2)) if c in "abef" else dma((2, CHIPS)) for c in "abcdefgh"},
        **{f"o{j}": dma((2, n)) for j, n in enumerate((8, 8, 7, 9))},
    }
    inputs = {
        "tok_in": (tokens, pl.ANY),
        "nbr_in": (nbr_embed, pl.ANY),
        "table": (neighbour_table.T, pltpu.SMEM),
        "counts": (valid_counts, pltpu.SMEM),
        "dec_in": (jnp.transpose(dec_proj, (1, 0, 2)), pl.ANY),
        "wq_in": (enc_query, pl.ANY),
        "wo_in": (enc_out, pl.ANY),
        "gain": (enc_gain, pltpu.VMEM),
        "wkv_in": (nbr_proj, pl.ANY),
        "wout_in": (out_proj, pl.ANY),
    }
    vmem = pl.BlockSpec(memory_space=pltpu.VMEM)
    names = (*inputs, "out_ref", "enc_ref", *scratch)
    results = pl.pallas_call(
        functools.partial(kernel, names),
        out_shape=(
            jax.ShapeDtypeStruct((rows, model), BF16),
            jax.ShapeDtypeStruct((NLEN, enc_width), BF16),
        ),
        in_specs=[pl.BlockSpec(memory_space=space) for _, space in inputs.values()],
        out_specs=(vmem, vmem),
        scratch_shapes=list(scratch.values()),
        compiler_params=pltpu.CompilerParams(
            collective_id=0, has_side_effects=True, vmem_limit_bytes=60 * 2**20
        ),
        name="retrieval",
    )(*(array for array, _ in inputs.values()))
    any_space = pl.BlockSpec(memory_space=pl.ANY)
    return pl.pallas_call(
        hand_out,
        out_shape=tuple(jax.ShapeDtypeStruct(a.shape, a.dtype) for a in results),
        in_specs=[vmem] * 2,
        out_specs=(any_space,) * 2,
        scratch_shapes=[dma((2,))],
        name="hand_out",
    )(*results)


def solution(mesh):
    return jax.shard_map(
        local,
        mesh=mesh,
        in_specs=(
            P(("seq", "nbr"), None),
            P("seq", "nbr", None),
            P("seq", None),
            P(),
            P(None, None, "nbr"),
            P(None, "nbr"),
            P("nbr", None),
            P(),
            P(None, None, "nbr"),
            P("nbr", None),
        ),
        out_specs=(P(("seq", "nbr"), None), P(("seq", "nbr"), None)),
        check_vma=False,
    )
```
